256 devices in a mesh: blk: 64 (over x_hi, z, y), tp: 4 (over x_lo, core).
Axes of the slice: x: 4 (x_hi: 2, x_lo: 2; x = x_hi * 2 + x_lo), y: 4, z: 8, core: 2. Of those that a mesh axis runs over, the one named last changes fastest.
Arguments:
- context_query_rows: bfloat16 [65536, 4096], P('blk', 'tp'), may hold values from -96 to 96
- context_key_rows: bfloat16 [65536, 1024], P('blk', 'tp'), may hold values from -8 to 8
- context_value_rows: bfloat16 [65536, 1024], P('blk', 'tp'), may hold values from -6 to 6
- block_lengths: int32 [64], replicated, may hold values from 512 to 1024, as said below
- scored_query_rows: bfloat16 [512, 4096], P('blk', 'tp'), may hold values from -96 to 96
- scored_positions: int32 [512], P('blk'), may hold values from 1024 to 65535, as said below
- out_weight: bfloat16 [4096, 4096], P('tp', 'blk'), may hold values from -0.09375 to 0.09375
Outputs:
- context_out: bfloat16 [65536, 4096], P('blk', 'tp')
- scored_out: bfloat16 [512, 4096], P('tp', 'blk')
The draws below stay inside these ranges and needn't reach their ends.
Inputs may be any that keep to these rules, and one draw needn't show every extreme that they name: `block_lengths`: each block has 512 to 1024 live tokens; at least one block is full. `scored_positions`: each position is a live token of a block other than block 0.
All inputs are finite; a program needn't handle non-finite values.
Results may differ from the reference program's by a relative error of at most 0.015.
Values may be sent and summed in bfloat16 or wider, within the bound.
A program may use at most 320 MiB of HBM per device.

```python
import math
import jax
import jax.numpy as jnp
from jax import lax

D = 4096
QUERY_HEADS = 32
KEY_VALUE_HEADS = 8
HEAD_SIZE = 128
BLOCK_TOKENS = 1024
CONTEXT_TOKENS = 65536
SCORED_QUERIES = 512


def length_table(key):
    block_count = CONTEXT_TOKENS // BLOCK_TOKENS
    drawn = jax.random.randint(jax.random.fold_in(key, 101), (block_count,), BLOCK_TOKENS // 2, BLOCK_TOKENS + 1)
    full_block = jax.random.randint(jax.random.fold_in(key, 102), (), 0, block_count)
    index_row = jnp.arange(block_count)
    return jnp.where((index_row == full_block) | (index_row == block_count - 1), BLOCK_TOKENS, drawn).astype(jnp.int32)


def position_table(key):
    block_count = CONTEXT_TOKENS // BLOCK_TOKENS
    live_lengths = length_table(key)
    blocks = jax.random.randint(jax.random.fold_in(key, 103), (SCORED_QUERIES,), 1, block_count)
    offsets = jax.random.randint(jax.random.fold_in(key, 104), (SCORED_QUERIES,), 0, BLOCK_TOKENS)
    offsets = offsets % live_lengths[blocks]
    positions = blocks * BLOCK_TOKENS + offsets
    index_row = jnp.arange(SCORED_QUERIES)
    positions = jnp.where(index_row == 0, BLOCK_TOKENS, positions)
    positions = jnp.where(index_row == SCORED_QUERIES - 1, CONTEXT_TOKENS - 1, positions)
    return positions.astype(jnp.int32)


def key_table(key):
    gaussian_sample = 1.5 * jax.random.normal(jax.random.fold_in(key, 105), (CONTEXT_TOKENS, KEY_VALUE_HEADS * HEAD_SIZE), jnp.float32)
    return jnp.clip(gaussian_sample, -8.0, 8.0)


def draw_block_lengths(key, part):
    return length_table(key)


def draw_scored_positions(key, part):
    return position_table(key)


def draw_context_key_rows(key, part):
    return key_table(key).astype(jnp.bfloat16)


def draw_context_query_rows(key, part):
    own_key = jax.random.fold_in(key, 7)
    gaussian_sample = jnp.clip(2.0 * jax.random.normal(own_key, (CONTEXT_TOKENS, QUERY_HEADS * HEAD_SIZE), jnp.float32), -10.0, 10.0)
    return gaussian_sample.astype(jnp.bfloat16)


def draw_scored_query_rows(key, part):
    own_key = jax.random.fold_in(key, 9)
    gaussian_sample = jnp.clip(2.0 * jax.random.normal(own_key, (SCORED_QUERIES, QUERY_HEADS * HEAD_SIZE), jnp.float32), -10.0, 10.0)
    return gaussian_sample.astype(jnp.bfloat16)


def block_scale(key, dims, shards, smallest, largest):
    level = 1.0
    for position, parts in shards:
        draws = jax.random.uniform(jax.random.fold_in(jax.random.fold_in(key, 6), position), (parts,), jnp.float32, smallest / len(shards), largest / len(shards))
        level = level * jnp.repeat(jnp.exp(draws), dims[position] // parts).reshape((-1,) + (1,) * (len(dims) - 1 - position))
    return level


def noise(rng, extent, spread, reach, cuts=(), held_as=jnp.bfloat16):
    values = jax.random.normal(rng, extent, jnp.float32) * spread
    if len(cuts) > 0:
        values = block_scale(rng, extent, cuts, -0.22, 0.18) * values
    return jnp.clip(values, min=-reach, max=reach).astype(held_as)


def setup_inputs(seed: int = 0) -> dict:
    arg_keys = jax.random.split(jax.random.key(seed), 8)
    return {
        "context_query_rows": draw_context_query_rows(jax.random.fold_in(arg_keys[7], 71), 0),
        "context_key_rows": draw_context_key_rows(jax.random.fold_in(arg_keys[7], 71), 0),
        "context_value_rows": noise(arg_keys[2], (CONTEXT_TOKENS, KEY_VALUE_HEADS * HEAD_SIZE), 1.0, 6.0, ((0, 64), (1, 4))),
        "block_lengths": draw_block_lengths(jax.random.fold_in(arg_keys[7], 71), 0),
        "scored_query_rows": draw_scored_query_rows(jax.random.fold_in(arg_keys[7], 71), 0),
        "scored_positions": draw_scored_positions(jax.random.fold_in(arg_keys[7], 71), 0),
        "out_weight": noise(arg_keys[6], (QUERY_HEADS * HEAD_SIZE, D), (QUERY_HEADS * HEAD_SIZE) ** -0.5, 0.09375, ((0, 4), (1, 64))),
    }


BLOCKED_SCORE = -1e+30

def attend(query_matrix, gathered_keys, gathered_values, allowed_mask):
    score_scale = 1.0 / math.sqrt(HEAD_SIZE)
    scores = jnp.einsum('rkgd,skd->rkgs', query_matrix, gathered_keys, precision=lax.Precision.HIGHEST) * score_scale
    allowed = allowed_mask[:, None, None, :]
    masked = jnp.where(allowed, scores, BLOCKED_SCORE)
    row_peak = lax.optimization_barrier(jnp.max(masked, axis=-1))
    weights = jnp.where(allowed, jnp.exp(masked - row_peak[..., None]), 0.0)
    weight_sum = lax.optimization_barrier(jnp.sum(weights, axis=-1))
    rounded = lax.optimization_barrier(weights.astype(jnp.bfloat16)).astype(jnp.float32)
    weighted = jnp.einsum('rkgs,skd->rkgd', rounded, gathered_values, precision=lax.Precision.HIGHEST)
    return (row_peak, weight_sum, weighted)

def reference(context_query_rows, context_key_rows, context_value_rows, block_lengths, scored_query_rows, scored_positions, out_weight):
    query_groups = QUERY_HEADS // KEY_VALUE_HEADS
    block_count = CONTEXT_TOKENS // BLOCK_TOKENS
    positions_local = jnp.arange(BLOCK_TOKENS, dtype=jnp.int32)
    anchor_keys = context_key_rows[:BLOCK_TOKENS].astype(jnp.float32).reshape(BLOCK_TOKENS, KEY_VALUE_HEADS, HEAD_SIZE)
    anchor_values = context_value_rows[:BLOCK_TOKENS].astype(jnp.float32).reshape(BLOCK_TOKENS, KEY_VALUE_HEADS, HEAD_SIZE)
    first_len = block_lengths[0]

    def context_block(block_index):
        starting_row = (block_index * BLOCK_TOKENS).astype(jnp.int32)
        query_matrix = lax.dynamic_slice_in_dim(context_query_rows, starting_row, BLOCK_TOKENS, 0).astype(jnp.float32).reshape(BLOCK_TOKENS, KEY_VALUE_HEADS, query_groups, HEAD_SIZE)
        local_keys = lax.dynamic_slice_in_dim(context_key_rows, starting_row, BLOCK_TOKENS, 0).astype(jnp.float32).reshape(BLOCK_TOKENS, KEY_VALUE_HEADS, HEAD_SIZE)
        local_values = lax.dynamic_slice_in_dim(context_value_rows, starting_row, BLOCK_TOKENS, 0).astype(jnp.float32).reshape(BLOCK_TOKENS, KEY_VALUE_HEADS, HEAD_SIZE)
        gathered_keys = jnp.concatenate([anchor_keys, local_keys], axis=0)
        gathered_values = jnp.concatenate([anchor_values, local_values], axis=0)
        own_len = block_lengths[block_index]
        anchor_live = (positions_local < first_len) & (block_index > 0)
        local_mask = (positions_local[None, :] <= positions_local[:, None]) & (positions_local[None, :] < own_len)
        allowed_mask = jnp.concatenate([jnp.broadcast_to(anchor_live[None, :], (BLOCK_TOKENS, BLOCK_TOKENS)), local_mask], axis=1)
        row_peak, weight_sum, weighted = attend(query_matrix, gathered_keys, gathered_values, allowed_mask)
        return (weighted / weight_sum[..., None]).reshape(BLOCK_TOKENS, QUERY_HEADS * HEAD_SIZE).astype(jnp.bfloat16)
    context_out = lax.map(context_block, jnp.arange(block_count, dtype=jnp.int32)).reshape(CONTEXT_TOKENS, QUERY_HEADS * HEAD_SIZE)
    query_matrix = scored_query_rows.astype(jnp.float32).reshape(SCORED_QUERIES, KEY_VALUE_HEADS, query_groups, HEAD_SIZE)

    def scan_block(carry, block_index):
        best_peak, merged_sums, merged_numer = carry
        starting_row = (block_index * BLOCK_TOKENS).astype(jnp.int32)
        gathered_keys = lax.dynamic_slice_in_dim(context_key_rows, starting_row, BLOCK_TOKENS, 0).astype(jnp.float32).reshape(BLOCK_TOKENS, KEY_VALUE_HEADS, HEAD_SIZE)
        gathered_values = lax.dynamic_slice_in_dim(context_value_rows, starting_row, BLOCK_TOKENS, 0).astype(jnp.float32).reshape(BLOCK_TOKENS, KEY_VALUE_HEADS, HEAD_SIZE)
        live = positions_local < block_lengths[block_index]
        allowed_mask = ((starting_row + positions_local)[None, :] <= scored_positions[:, None]) & live[None, :]
        row_peak, weight_sum, weighted = attend(query_matrix, gathered_keys, gathered_values, allowed_mask)
        new_peak = jnp.maximum(best_peak, row_peak)
        older = jnp.exp(best_peak - new_peak)
        fresh = jnp.exp(row_peak - new_peak)
        merged_sums = merged_sums * older + weight_sum * fresh
        merged_numer = merged_numer * older[..., None] + weighted * fresh[..., None]
        return ((new_peak, merged_sums, merged_numer), None)
    starting_carry = (jnp.full((SCORED_QUERIES, KEY_VALUE_HEADS, query_groups), BLOCKED_SCORE, jnp.float32), jnp.zeros((SCORED_QUERIES, KEY_VALUE_HEADS, query_groups), jnp.float32), jnp.zeros((SCORED_QUERIES, KEY_VALUE_HEADS, query_groups, HEAD_SIZE), jnp.float32))
    (best_peak, merged_sums, merged_numer), unused = lax.scan(scan_block, starting_carry, jnp.arange(block_count, dtype=jnp.int32))
    attended = (merged_numer / merged_sums[..., None]).reshape(SCORED_QUERIES, QUERY_HEADS * HEAD_SIZE).astype(jnp.bfloat16)
    scored_out = jnp.dot(attended, out_weight, preferred_element_type=jnp.float32).astype(jnp.bfloat16)
    return (context_out, scored_out)
```

```python
import functools
import math

import jax
import jax.numpy as jnp
from jax import lax
from jax.experimental import pallas as pl
from jax.experimental.pallas import tpu as pltpu
from jax.sharding import PartitionSpec as P

BT = 1024
HEAD = 128
TOK = 8
PIECE = 4 * TOK
LOG2_SCALE = math.log2(math.e) / math.sqrt(HEAD)
NEG = -1e30
CHUNK = 256
TILE = 256
ROWS = 4 * TILE
MESH = pl.DeviceIdType.MESH
F32 = jnp.float32
BF16 = jnp.bfloat16


def dot_t(a, b):
    return lax.dot_general(a, b, (((1,), (1,)), ((), ())), preferred_element_type=F32)


def expand_keys(keys, values, live_len, filler_ref, kx, vx):
    live = lax.broadcasted_iota(jnp.int32, (BT, HEAD), 0) < live_len
    for g in range(2):
        cols = slice(g * HEAD, (g + 1) * HEAD)
        scaled = jnp.where(live, keys[:, cols].astype(F32), filler_ref[0:16, cols].astype(F32)[0:1]) * LOG2_SCALE
        high = scaled.astype(BF16)
        kx[g, :, 0:HEAD] = high
        kx[g, :, HEAD : 2 * HEAD] = (scaled - high.astype(F32)).astype(BF16)
        vx[g, :, 0:HEAD] = jnp.where(live, values[:, cols].astype(F32), 0.0).astype(BF16)
        vx[g, :, HEAD : 2 * HEAD] = jnp.where(live, 1.0, 0.0).astype(BF16)


def fold_max(m, s):
    for j in range(0, s.shape[1], HEAD):
        m = jnp.maximum(m, s[:, j : j + HEAD])
    return m


def context_queries(q_ref, g, r0):
    parts = [
        q_ref[r0 : r0 + TILE, pl.ds(pl.multiple_of(g * 512 + h * HEAD, HEAD), HEAD)] for h in range(4)
    ]
    q = jnp.concatenate(parts, axis=0)
    return jnp.concatenate([q, q], axis=1)


class Sems:
    def __init__(self, send, recv):
        self.send, self.recv, self.used = send, recv, 0

    def take(self):
        i = self.used
        self.used += 1
        return i


def merge(lses):
    best = functools.reduce(jnp.maximum, lses)
    terms = [jnp.exp2(l - best) for l in lses]
    total = functools.reduce(jnp.add, terms)
    return [t / total for t in terms], best + jnp.log2(total)


def lane_weights(w, lane):
    return jnp.concatenate(
        [jnp.broadcast_to(w[:, lane + h : lane + h + 1], (TOK, HEAD)) for h in range(4)], axis=0
    )


def kernel(
    dims,
    lengths,
    positions,
    q_hbm,
    k_hbm,
    v_hbm,
    qs_ref,
    w_ref,
    ctx_hbm,
    out_ref,
    q_ref,
    k_ref,
    v_ref,
    out_buf,
    kx,
    vx,
    akx,
    avx,
    s_buf,
    own_acc,
    own_peak,
    qa,
    qb,
    pos,
    ak,
    av,
    o0,
    o1,
    st0,
    st1,
    r0y,
    t0y,
    r1x,
    t1x,
    o0x,
    l0x,
    r0x,
    t0x,
    o1y,
    l1y,
    r1y,
    t1y,
    oz,
    lz,
    rz,
    tz,
    aa,
    ab,
    proj,
    rproj,
    send_sems,
    recv_sems,
    local_sems,
):
    NX, NZ, NY, NT = dims
    NB = NX * NZ * NY
    blk = lax.axis_index("blk")
    tp = lax.axis_index("tp")
    xh = blk // (NZ * NY)
    z = ((blk // NY) % NZ)
    y = ((blk) % NY)
    is_root = blk == 0
    other = NX - 1 - xh

    def at_x(v):
        return v * (NZ * NY) + z * NY + y

    def at_z(v):
        return xh * (NZ * NY) + v * NY + y

    def at_y(v):
        return xh * (NZ * NY) + z * NY + v

    zs = [((z + i) % NZ) for i in range(NZ)]
    ys = [((y + i) % NY) for i in range(NY)]
    zb = [((z + NZ - i) % NZ) for i in range(NZ)]
    yb = [((y + NY - i) % NY) for i in range(NY)]
    sems = Sems(send_sems, recv_sems)

    loads = [
        pltpu.make_async_copy(k_hbm, k_ref, local_sems.at[0]),
        pltpu.make_async_copy(v_hbm, v_ref, local_sems.at[1]),
        pltpu.make_async_copy(q_hbm, q_ref, local_sems.at[2]),
    ]
    for c in loads:
        c.start()

    barrier = pltpu.get_barrier_semaphore()

    def greet(device):
        pl.semaphore_signal(barrier, inc=1, device_id=device, device_id_type=MESH)

    for i in range(1, NZ):
        greet({"blk": at_z(zs[i])})
    for i in range(1, NY):
        greet({"blk": at_y(ys[i])})
    greet({"blk": at_x(other)})
    for i in range(1, NT):
        greet({"tp": ((tp + i) % NT)})

    @pl.when(jnp.logical_not(is_root))
    def _():
        greet({"blk": 0})

    near = NZ - 1 + NY - 1 + 1 + NT - 1

    def copy(src, dst, pair, device):
        return pltpu.make_async_remote_copy(
            src_ref=src, dst_ref=dst, send_sem=send_sems.at[pair], recv_sem=recv_sems.at[pair], device_id=device, device_id_type=MESH
        )

    sent = []

    def start(make):
        make().start()
        sent.append(make)

    class Gather:
        def __init__(self, a, b, extra=()):
            self.a, self.b = a, b
            self.first = tuple([a, b]) + tuple(extra)
            self.via_x = tuple([a]) + tuple(extra)
            self.p_z = [[sems.take() for _ in self.first] for _ in range(1, NZ)]
            self.p_ax = [sems.take() for _ in self.via_x]
            self.p_by = [sems.take() for _ in range(1, NY)]
            self.p_ay = [[sems.take() for _ in self.via_x] for _ in range(1, NY)]
            self.p_bx = sems.take()

        def start_z(self):
            for i in range(1, NZ):
                for ref, pair in zip(self.first, self.p_z[i - 1]):
                    start(lambda ref=ref, pair=pair, i=i: copy(ref.at[xh, z, y], ref.at[xh, z, y], pair, {"blk": at_z(zs[i])}))

        def wait_z(self):
            for i in range(1, NZ):
                for ref, pair in zip(self.first, self.p_z[i - 1]):
                    slot = ref.at[xh, zb[i], y]
                    copy(slot, slot, pair, {"blk": at_z(zs[i])}).wait_recv()

        def start_2(self):
            for ref, pair in zip(self.via_x, self.p_ax):
                start(lambda ref=ref, pair=pair: copy(ref.at[xh, :, y], ref.at[xh, :, y], pair, {"blk": at_x(other)}))
            for i in range(1, NY):
                start(lambda i=i: copy(self.b.at[xh, :, y], self.b.at[xh, :, y], self.p_by[i - 1], {"blk": at_y(ys[i])}))

        def wait_2(self):
            for ref, pair in zip(self.via_x, self.p_ax):
                slot = ref.at[other, :, y]
                copy(slot, slot, pair, {"blk": at_x(other)}).wait_recv()
            for i in range(1, NY):
                slot = self.b.at[xh, :, yb[i]]
                copy(slot, slot, self.p_by[i - 1], {"blk": at_y(ys[i])}).wait_recv()

        def start_3(self):
            for i in range(1, NY):
                for ref, pair in zip(self.via_x, self.p_ay[i - 1]):
                    start(lambda ref=ref, pair=pair, i=i: copy(ref.at[:, :, y], ref.at[:, :, y], pair, {"blk": at_y(ys[i])}))
            start(lambda: copy(self.b.at[xh], self.b.at[xh], self.p_bx, {"blk": at_x(other)}))

        def wait_3y(self, i):
            for ref, pair in zip(self.via_x, self.p_ay[i - 1]):
                slot = ref.at[:, :, yb[i]]
                copy(slot, slot, pair, {"blk": at_y(ys[i])}).wait_recv()

        def wait_3x(self):
            slot = self.b.at[other]
            copy(slot, slot, self.p_bx, {"blk": at_x(other)}).wait_recv()

    gather_q = Gather(qa, qb, (pos,))
    gather_kv = Gather(ak, av)
    gather_att = Gather(aa, ab)
    scatter = [sems.take() for _ in range(2)]
    p_y0 = [(sems.take(), sems.take()) for _ in range(1, NY)]
    p_x1 = [(sems.take(), sems.take())]
    p_x0 = [(sems.take(), sems.take())]
    p_y1 = [(sems.take(), sems.take()) for _ in range(1, NY)]
    p_z01 = [(sems.take(), sems.take()) for _ in range(1, NZ)]
    p_tp = [sems.take() for _ in range(1, NT)]

    q_piece = qs_ref[...].astype(F32)
    for g, ref in ((0, qa), (1, qb)):
        ref[xh, z, y] = jnp.concatenate(
            [q_piece[:, (g * 4 + h) * HEAD : (g * 4 + h + 1) * HEAD] for h in range(4)], axis=0
        ).astype(BF16)
    row = lax.broadcasted_iota(jnp.int32, (TOK, HEAD), 0)
    tile = jnp.zeros((TOK, HEAD), jnp.int32)
    for i in range(TOK):
        tile = jnp.where(row == i, positions[i], tile)
    pos[xh, z, y] = tile

    loads[0].wait()
    loads[1].wait()
    pl.semaphore_wait(barrier, near + jnp.where(is_root, NB - 1, 0))
    gather_q.start_z()

    share = BT // NB

    @pl.when(is_root)
    def _():
        ak[0, 0, 0] = k_ref[0:share, :]
        av[0, 0, 0] = v_ref[0:share, :]

        def hand(d, carry):
            rows = pl.ds(pl.multiple_of(d * share, share), share)
            dx, dz, dy = d // (NZ * NY), ((d // NY) % NZ), ((d) % NY)
            copy(k_ref.at[rows], ak.at[dx, dz, dy], scatter[0], {"blk": d}).start()
            copy(v_ref.at[rows], av.at[dx, dz, dy], scatter[1], {"blk": d}).start()
            return carry

        lax.fori_loop(1, NB, hand, 0)

    own_len = lengths[blk]
    anchor_len = jnp.where(is_root, 0, lengths[0])
    expand_keys(k_ref[...], v_ref[...], own_len, k_ref, kx, vx)
    loads[2].wait()

    def own_group(g, carry):
        prev = None
        for t in range(BT // TILE + 1):
            r0 = t * TILE
            here = t < BT // TILE
            if here:
                q = context_queries(q_ref, g, r0)
                m = jnp.full((ROWS, HEAD), NEG, F32)
            if prev is not None:
                acc = jnp.zeros((ROWS, 2 * HEAD), F32)
            for c in range(BT // CHUNK):
                cols = slice(c * CHUNK, (c + 1) * CHUNK)
                if here and c <= t:
                    s = dot_t(q, kx[g, cols, :])
                    if c == t:
                        i = lax.broadcasted_iota(jnp.int32, (4, TILE, CHUNK), 1).reshape(ROWS, CHUNK)
                        j = lax.broadcasted_iota(jnp.int32, (ROWS, CHUNK), 1)
                        s = jnp.where(j <= i, s, NEG)
                    s_buf[t % 2, :, cols] = s
                    m = fold_max(m, s)
                if prev is not None and c <= t - 1:
                    p = jnp.exp2(s_buf[(t - 1) % 2, :, cols] - prev).astype(BF16)
                    acc += jnp.dot(p, vx[g, cols, :], preferred_element_type=F32)
            if prev is not None:
                own_acc[g * 4 + t - 1] = acc
                own_peak[g * 4 + t - 1] = jnp.broadcast_to(prev, (ROWS, HEAD))
            if here:
                prev = jnp.max(m, axis=1, keepdims=True)

        @pl.when(g == 0)
        def _():
            gather_q.wait_z()
            gather_q.start_2()

        return carry

    lax.fori_loop(0, 2, own_group, 0)
    gather_q.wait_2()
    gather_q.start_3()

    @pl.when(jnp.logical_not(is_root))
    def _():
        copy(k_ref.at[0:share], ak.at[xh, z, y], scatter[0], {"blk": 0}).wait_recv()
        copy(v_ref.at[0:share], av.at[xh, z, y], scatter[1], {"blk": 0}).wait_recv()

    gather_kv.start_z()

    lane = lax.broadcasted_iota(jnp.int32, (TOK, HEAD), 1)
    dev0 = NX * NZ
    halves = NY // NX
    dev1 = NZ * NY // halves
    zpart = NZ // halves
    rows0 = dev0 * PIECE
    rows1 = dev1 * PIECE

    def scored_scores(q, limits, g, slot, count):
        rows = count * PIECE
        q = jnp.concatenate([q, q], axis=1)
        limits = jnp.concatenate([limits, limits], axis=2) - blk * BT
        m = jnp.full((rows, HEAD), NEG, F32)
        for c in range(BT // CHUNK):
            cols = slice(c * CHUNK, (c + 1) * CHUNK)
            s = dot_t(q, kx[g, cols, :]).reshape(count, 4, TOK, CHUNK)
            col = c * CHUNK + lax.broadcasted_iota(jnp.int32, (count, TOK, CHUNK), 2)
            ok = jnp.broadcast_to((col <= limits)[:, None], (count, 4, TOK, CHUNK))
            s = jnp.where(ok, s, NEG).reshape(rows, CHUNK)
            s_buf[slot, 0:rows, cols] = s
            m = fold_max(m, s)
        return jnp.max(m, axis=1, keepdims=True)

    def scored_values(peak, g, slot, count):
        rows = count * PIECE
        acc = jnp.zeros((rows, 2 * HEAD), F32)
        for c in range(BT // CHUNK):
            cols = slice(c * CHUNK, (c + 1) * CHUNK)
            p = jnp.exp2(s_buf[slot, 0:rows, cols] - peak).astype(BF16)
            acc += jnp.dot(p, vx[g, cols, :], preferred_element_type=F32)
        sums = acc[:, HEAD:]
        lse = (peak + jnp.log2(sums)).reshape(count, 4, TOK, HEAD)
        return (acc[:, :HEAD] / sums).astype(BF16), lse

    def stat_tile(lse, limits, devices, offsets):
        out = jnp.full((TOK, HEAD), NEG, F32)
        for d, offset in zip(devices, offsets):
            for h in range(4):
                out = jnp.where((lane == offset + h) & (limits[d] >= blk * BT), lse[d, h], out)
        return out

    for i in range(NY):
        yi = yb[i]
        xi = xh if i < halves else other
        z0 = (i % halves) * zpart
        if i > 0:
            gather_q.wait_3y(i)
        if i == halves:
            gather_q.wait_3x()
        q0 = qa[:, :, yi].reshape(rows0, HEAD)
        lim0 = pos[:, :, yi].reshape(dev0, TOK, HEAD)
        peak0 = scored_scores(q0, lim0, 0, 0, dev0)
        out0, lse0 = scored_values(peak0, 0, 0, dev0)
        o0[yi] = out0.reshape(NX, NZ, PIECE, HEAD)
        st0[yi] = stat_tile(
            lse0, lim0, range(dev0), [(d // NZ) * 64 + (d % NZ) * 8 for d in range(dev0)]
        )
        if i > 0:
            pairs = p_y0[NY - i - 1]
            start(lambda i=i, yi=yi, pair=pairs[0]: copy(o0.at[yi], r0y.at[NY - i - 1], pair, {"blk": at_y(yi)}))
            start(lambda i=i, yi=yi, pair=pairs[1]: copy(st0.at[yi], t0y.at[NY - i - 1], pair, {"blk": at_y(yi)}))
    for i in range(NY):
        xi = xh if i < halves else other
        z0 = (i % halves) * zpart
        q1 = qb[xi, z0 : z0 + zpart].reshape(rows1, HEAD)
        lim1 = pos[xi, z0 : z0 + zpart].reshape(dev1, TOK, HEAD)
        peak1 = scored_scores(q1, lim1, 1, 1, dev1)
        out1, lse1 = scored_values(peak1, 1, 1, dev1)
        o1[xi, z0 : z0 + zpart] = out1.reshape(zpart, NY, PIECE, HEAD)
        for yy in range(NY):
            devices = [zz * NY + yy for zz in range(zpart)]
            new = stat_tile(lse1, lim1, devices, [(z0 + zz) * 8 for zz in range(zpart)])
            if i % halves == 0:
                st1[xi, yy] = new
            else:
                st1[xi, yy] = jnp.maximum(st1[xi, yy], new)
    start(lambda: copy(o1.at[other], r1x, p_x1[0][0], {"blk": at_x(other)}))
    start(lambda: copy(st1.at[other], t1x, p_x1[0][1], {"blk": at_x(other)}))

    gather_kv.wait_z()
    gather_kv.start_2()

    def sums_1():
        for i in range(1, NY):
            copy(o0.at[y], r0y.at[i - 1], p_y0[i - 1][0], {"blk": at_y(ys[i])}).wait_recv()
            copy(st0.at[y], t0y.at[i - 1], p_y0[i - 1][1], {"blk": at_y(ys[i])}).wait_recv()
        ws, l0x[...] = merge([st0[y]] + [t0y[i] for i in range(NY - 1)])
        for a in range(NX):
            for b in range(NZ):
                at = a * 64 + b * 8
                total = o0[y, a, b].astype(F32) * lane_weights(ws[0], at)
                for i in range(NY - 1):
                    total += r0y[i, a, b].astype(F32) * lane_weights(ws[i + 1], at)
                o0x[a, b] = total.astype(BF16)
        start(lambda: copy(o0x.at[other], r0x, p_x0[0][0], {"blk": at_x(other)}))
        start(lambda: copy(l0x, t0x, p_x0[0][1], {"blk": at_x(other)}))
        copy(o1.at[xh], r1x, p_x1[0][0], {"blk": at_x(other)}).wait_recv()
        copy(st1.at[xh], t1x, p_x1[0][1], {"blk": at_x(other)}).wait_recv()
        for c in range(NY):
            ws, l1y[c] = merge([st1[xh, c], t1x[c]])
            for b in range(NZ):
                total = o1[xh, b, c].astype(F32) * lane_weights(ws[0], b * 8)
                total += r1x[b, c].astype(F32) * lane_weights(ws[1], b * 8)
                o1y[c, b] = total.astype(BF16)
        for i in range(1, NY):
            start(lambda i=i: copy(o1y.at[ys[i]], r1y.at[i - 1], p_y1[i - 1][0], {"blk": at_y(ys[i])}))
            start(lambda i=i: copy(l1y.at[ys[i]], t1y.at[i - 1], p_y1[i - 1][1], {"blk": at_y(ys[i])}))

    def sums_2():
        copy(o0x.at[xh], r0x, p_x0[0][0], {"blk": at_x(other)}).wait_recv()
        copy(l0x, t0x, p_x0[0][1], {"blk": at_x(other)}).wait_recv()

        def own_x(t):
            return jnp.where(xh == 0, t, pltpu.roll(t, 64, 1))

        ws, lse = merge([own_x(l0x[...]), own_x(t0x[...])])
        lz[0] = lse
        for b in range(NZ):
            total = o0x[xh, b].astype(F32) * lane_weights(ws[0], b * 8)
            total += r0x[b].astype(F32) * lane_weights(ws[1], b * 8)
            oz[b, 0] = total.astype(BF16)
        for i in range(1, NY):
            copy(o1y.at[y], r1y.at[i - 1], p_y1[i - 1][0], {"blk": at_y(ys[i])}).wait_recv()
            copy(l1y.at[y], t1y.at[i - 1], p_y1[i - 1][1], {"blk": at_y(ys[i])}).wait_recv()
        ws, lse = merge([l1y[y]] + [t1y[i] for i in range(NY - 1)])
        lz[1] = lse
        for b in range(NZ):
            total = o1y[y, b].astype(F32) * lane_weights(ws[0], b * 8)
            for i in range(NY - 1):
                total += r1y[i, b].astype(F32) * lane_weights(ws[i + 1], b * 8)
            oz[b, 1] = total.astype(BF16)
        for i in range(1, NZ):
            start(lambda i=i: copy(oz.at[zs[i]], rz.at[i - 1], p_z01[i - 1][0], {"blk": at_z(zs[i])}))
            start(lambda i=i: copy(lz, tz.at[i - 1], p_z01[i - 1][1], {"blk": at_z(zs[i])}))

    def sums_3():
        for i in range(1, NZ):
            copy(oz.at[z], rz.at[i - 1], p_z01[i - 1][0], {"blk": at_z(zs[i])}).wait_recv()
            copy(lz, tz.at[i - 1], p_z01[i - 1][1], {"blk": at_z(zs[i])}).wait_recv()
        for g, ref in ((0, aa), (1, ab)):
            ws, _ = merge([lz[g]] + [tz[i, g] for i in range(NZ - 1)])
            total = jnp.zeros((PIECE, HEAD), F32)
            for i in range(NZ):
                part = oz[z, g] if i == 0 else rz[i - 1, g]
                factor = jnp.concatenate(
                    [
                        jnp.broadcast_to(
                            jnp.sum(jnp.where(lane == z * 8 + h, ws[i], 0.0), axis=1, keepdims=True), (TOK, HEAD)
                        )
                        for h in range(4)
                    ],
                    axis=0,
                )
                total += part.astype(F32) * factor
            ref[xh, z, y] = total.astype(BF16)
        gather_att.start_z()

    gather_kv.wait_2()
    gather_kv.start_3()
    for i in range(1, NY):
        gather_kv.wait_3y(i)
    gather_kv.wait_3x()
    expand_keys(ak[...].reshape(BT, 2 * HEAD), av[...].reshape(BT, 2 * HEAD), anchor_len, k_ref, akx, avx)

    def anchor_group(g, carry):
        prev = None
        for t in range(BT // TILE + 1):
            r0 = t * TILE
            here = t < BT // TILE
            if here:
                q = context_queries(q_ref, g, r0)
                m = own_peak[g * 4 + t]
            if prev is not None:
                before = own_peak[g * 4 + t - 1]
                fade = jnp.exp2(before - prev)
                acc = own_acc[g * 4 + t - 1] * jnp.concatenate([fade, fade], axis=1)
            for c in range(BT // CHUNK):
                cols = slice(c * CHUNK, (c + 1) * CHUNK)
                if here:
                    s = dot_t(q, akx[g, cols, :])
                    s_buf[t % 2, :, cols] = s
                    m = fold_max(m, s)
                if prev is not None:
                    p = jnp.exp2(s_buf[(t - 1) % 2, :, cols] - prev).astype(BF16)
                    acc += jnp.dot(p, avx[g, cols, :], preferred_element_type=F32)
            if prev is not None:
                out = (acc[:, :HEAD] / acc[:, HEAD:]).astype(BF16)
                for h in range(4):
                    out_buf[g, (t - 1) * TILE : t * TILE, h * HEAD : (h + 1) * HEAD] = out[
                        h * TILE : (h + 1) * TILE
                    ]
            if here:
                prev = jnp.max(m, axis=1, keepdims=True)

        @pl.when(g == 0)
        def _():
            sums_1()

        return carry

    lax.fori_loop(0, 2, anchor_group, 0)
    stores = [
        pltpu.make_async_copy(out_buf.at[g], ctx_hbm.at[:, g * 512 : (g + 1) * 512], local_sems.at[3 + g])
        for g in range(2)
    ]
    for c in stores:
        c.start()
    sums_2()
    sums_3()
    gather_att.wait_z()
    gather_att.start_2()
    gather_att.wait_2()
    gather_att.start_3()
    for i in range(1, NY):
        gather_att.wait_3y(i)
    gather_att.wait_3x()

    total = jnp.zeros((NB, TOK, HEAD), F32)
    for g, ref in ((0, aa), (1, ab)):
        weights = jnp.concatenate(
            [w_ref[(g * 4 + h) * HEAD : (g * 4 + h + 1) * HEAD, :] for h in range(4)], axis=1
        )
        full = jnp.dot(ref[...].reshape(NB * PIECE, HEAD), weights, preferred_element_type=F32)
        full = full.reshape(NB, 4, TOK, 2 * HEAD)
        low = full[:, 0, :, :HEAD] + full[:, 2, :, HEAD:]
        high = full[:, 1, :, :HEAD] + full[:, 3, :, HEAD:]
        total += jnp.where(lax.broadcasted_iota(jnp.int32, (NB, TOK, HEAD), 2) < 64, low, high)
    total = total.reshape(NB * TOK, HEAD)
    total = total + pltpu.roll(total, 64, 1)
    per = NB * TOK // NT
    half = per // 2
    first = lax.broadcasted_iota(jnp.int32, (half, HEAD), 1) < 64
    for t in range(NT):
        proj[t] = jnp.where(first, total[t * per : t * per + half], total[t * per + half : (t + 1) * per]).astype(BF16)
    for i in range(1, NT):
        to = ((tp + i) % NT)
        start(lambda i=i, to=to: copy(proj.at[to], rproj.at[i - 1], p_tp[i - 1], {"tp": to}))
    result = proj[tp].astype(F32)
    for i in range(1, NT):
        copy(proj.at[tp], rproj.at[i - 1], p_tp[i - 1], {"tp": ((tp + i) % NT)}).wait_recv()
        result += rproj[i - 1].astype(F32)
    result = result.astype(BF16)
    out_ref[0:half, :] = result[:, 0:64]
    out_ref[half:per, :] = result[:, 64:128]

    for make in sent:
        make().wait_send()

    @pl.when(is_root)
    def _():
        def settle(d, carry):
            copy(k_ref.at[0:share], ak.at[0, 0, 0], scatter[0], {"blk": d}).wait_send()
            copy(v_ref.at[0:share], av.at[0, 0, 0], scatter[1], {"blk": d}).wait_send()
            return carry

        lax.fori_loop(1, NB, settle, 0)

    for c in stores:
        c.wait()


def solution(mesh, dims=(2, 8, 4, 4)):
    NX, NZ, NY, NT = dims
    NB = NX * NZ * NY
    vmem = pl.BlockSpec(memory_space=pltpu.VMEM)
    smem = pl.BlockSpec(memory_space=pltpu.SMEM)
    hbm = pl.BlockSpec(memory_space=pl.ANY)
    pieces = (NX, NZ, NY, PIECE, HEAD)
    anchor = (NX, NZ, NY, BT // NB, 2 * HEAD)
    per = NB * TOK // NT

    def local(q, k, v, lengths, q_scored, positions, weight):
        call = pl.pallas_call(
            functools.partial(kernel, dims),
            out_shape=(
                jax.ShapeDtypeStruct((BT, 1024), BF16),
                jax.ShapeDtypeStruct((per, 64), BF16),
            ),
            in_specs=[smem, smem, hbm, hbm, hbm, vmem, vmem],
            out_specs=(hbm, vmem),
            scratch_shapes=[
                pltpu.VMEM((BT, 1024), BF16),
                pltpu.VMEM((BT, 2 * HEAD), BF16),
                pltpu.VMEM((BT, 2 * HEAD), BF16),
                pltpu.VMEM((2, BT, 512), BF16),
                pltpu.VMEM((2, BT, 2 * HEAD), BF16),
                pltpu.VMEM((2, BT, 2 * HEAD), BF16),
                pltpu.VMEM((2, BT, 2 * HEAD), BF16),
                pltpu.VMEM((2, BT, 2 * HEAD), BF16),
                pltpu.VMEM((2, ROWS, BT), F32),
                pltpu.VMEM((8, ROWS, 2 * HEAD), F32),
                pltpu.VMEM((8, ROWS, HEAD), F32),
                pltpu.VMEM(pieces, BF16),
                pltpu.VMEM(pieces, BF16),
                pltpu.VMEM((NX, NZ, NY, TOK, HEAD), jnp.int32),
                pltpu.VMEM(anchor, BF16),
                pltpu.VMEM(anchor, BF16),
                pltpu.VMEM((NY, NX, NZ, PIECE, HEAD), BF16),
                pltpu.VMEM((NX, NZ, NY, PIECE, HEAD), BF16),
                pltpu.VMEM((NY, TOK, HEAD), F32),
                pltpu.VMEM((NX, NY, TOK, HEAD), F32),
                pltpu.VMEM((NY - 1, NX, NZ, PIECE, HEAD), BF16),
                pltpu.VMEM((NY - 1, TOK, HEAD), F32),
                pltpu.VMEM((NZ, NY, PIECE, HEAD), BF16),
                pltpu.VMEM((NY, TOK, HEAD), F32),
                pltpu.VMEM((NX, NZ, PIECE, HEAD), BF16),
                pltpu.VMEM((TOK, HEAD), F32),
                pltpu.VMEM((NZ, PIECE, HEAD), BF16),
                pltpu.VMEM((TOK, HEAD), F32),
                pltpu.VMEM((NY, NZ, PIECE, HEAD), BF16),
                pltpu.VMEM((NY, TOK, HEAD), F32),
                pltpu.VMEM((NY - 1, NZ, PIECE, HEAD), BF16),
                pltpu.VMEM((NY - 1, TOK, HEAD), F32),
                pltpu.VMEM((NZ, 2, PIECE, HEAD), BF16),
                pltpu.VMEM((2, TOK, HEAD), F32),
                pltpu.VMEM((NZ - 1, 2, PIECE, HEAD), BF16),
                pltpu.VMEM((NZ - 1, 2, TOK, HEAD), F32),
                pltpu.VMEM(pieces, BF16),
                pltpu.VMEM(pieces, BF16),
                pltpu.VMEM((NT, per // 2, HEAD), BF16),
                pltpu.VMEM((NT - 1, per // 2, HEAD), BF16),
                pltpu.SemaphoreType.DMA((160,)),
                pltpu.SemaphoreType.DMA((160,)),
                pltpu.SemaphoreType.DMA((5,)),
            ],
            compiler_params=pltpu.CompilerParams(
                collective_id=0, has_side_effects=True, vmem_limit_bytes=60 * 2**20
            ),
            name="star_attention",
        )
        return call(lengths, positions, q, k, v, q_scored, weight)

    in_specs = (P("blk", "tp"), P("blk", "tp"), P("blk", "tp"), P(), P("blk", "tp"), P("blk"), P("tp", "blk"))
    out_specs = (P("blk", "tp"), P("tp", "blk"))
    return jax.shard_map(local, mesh=mesh, in_specs=in_specs, out_specs=out_specs, check_vma=False)
```

```python
import functools
import math

import jax
import jax.numpy as jnp
from jax import lax
from jax.experimental import pallas as pl
from jax.experimental.pallas import tpu as pltpu
from jax.sharding import PartitionSpec as P

BT = 1024
HEAD = 128
TOK = 8
PIECE = 4 * TOK
LOG2_SCALE = math.log2(math.e) / math.sqrt(HEAD)
NEG = -1e30
CHUNK = 256
TILE = 256
ROWS = 4 * TILE
MESH = pl.DeviceIdType.MESH
F32 = jnp.float32
BF16 = jnp.bfloat16


def dot_t(a, b):
    return lax.dot_general(a, b, (((1,), (1,)), ((), ())), preferred_element_type=F32)


def expand_keys(keys, values, live_len, filler_ref, kx, vx):
    live = lax.broadcasted_iota(jnp.int32, (BT, HEAD), 0) < live_len
    for g in range(2):
        cols = slice(g * HEAD, (g + 1) * HEAD)
        scaled = jnp.where(live, keys[:, cols].astype(F32), filler_ref[0:16, cols].astype(F32)[0:1]) * LOG2_SCALE
        high = scaled.astype(BF16)
        kx[g, :, 0:HEAD] = high
        kx[g, :, HEAD : 2 * HEAD] = (scaled - high.astype(F32)).astype(BF16)
        vx[g, :, 0:HEAD] = jnp.where(live, values[:, cols].astype(F32), 0.0).astype(BF16)
        vx[g, :, HEAD : 2 * HEAD] = jnp.where(live, 1.0, 0.0).astype(BF16)


def fold_max(m, s):
    for j in range(0, s.shape[1], HEAD):
        m = jnp.maximum(m, s[:, j : j + HEAD])
    return m


def context_queries(q_ref, g, r0):
    parts = [
        q_ref[r0 : r0 + TILE, pl.ds(pl.multiple_of(g * 512 + h * HEAD, HEAD), HEAD)] for h in range(4)
    ]
    q = jnp.concatenate(parts, axis=0)
    return jnp.concatenate([q, q], axis=1)


class Sems:
    def __init__(self, send, recv):
        self.send, self.recv, self.used = send, recv, 0

    def take(self):
        i = self.used
        self.used += 1
        return i


def merge(lses):
    best = functools.reduce(jnp.maximum, lses)
    terms = [jnp.exp2(l - best) for l in lses]
    total = functools.reduce(jnp.add, terms)
    return [t / total for t in terms], best + jnp.log2(total)


def lane_weights(w, lane):
    return jnp.concatenate(
        [jnp.broadcast_to(w[:, lane + h : lane + h + 1], (TOK, HEAD)) for h in range(4)], axis=0
    )


def kernel(
    dims,
    lengths_hbm,
    positions_hbm,
    q_hbm,
    k_hbm,
    v_hbm,
    qs_hbm,
    w_hbm,
    ctx_hbm,
    out_ref,
    lengths,
    positions,
    qs_ref,
    q_ref,
    k_ref,
    v_ref,
    out_buf,
    kx,
    vx,
    akx,
    avx,
    s_buf,
    own_acc,
    own_peak,
    qz,
    qa,
    qb,
    pos,
    pos1,
    ak,
    av,
    o0,
    o1,
    st0,
    st1,
    r0y,
    t0y,
    r1x,
    t1x,
    o0x,
    l0x,
    r0x,
    t0x,
    o1y,
    l1y,
    r1y,
    t1y,
    oz,
    lz,
    rz,
    tz,
    att,
    wt,
    msg,
    got,
    send_sems,
    recv_sems,
    local_sems,
):
    NX, NZ, NY, NT = dims
    NB = NX * NZ * NY
    blk = lax.axis_index("blk")
    tp = lax.axis_index("tp")
    xh = lax.div(blk, NZ * NY)
    z = lax.rem(lax.div(blk, NY), NZ)
    y = lax.rem(blk, NY)
    is_root = blk == 0
    HT = NT // NX
    ZH = NZ // HT
    other = NX - 1 - xh

    def at_x(v):
        return v * (NZ * NY) + z * NY + y

    def at_z(v):
        return xh * (NZ * NY) + v * NY + y

    def at_y(v):
        return xh * (NZ * NY) + z * NY + v

    def at_xy(dx, dy):
        return xs[dx] * (NZ * NY) + z * NY + ys[dy]

    xs = [xh, NX - 1 - xh]
    zs = [z] + [lax.rem(z + i, NZ) for i in range(1, NZ)]
    ys = [y] + [lax.rem(y + i, NY) for i in range(1, NY)]
    zb = [zs[(NZ - i) % NZ] for i in range(NZ)]
    yb = [ys[(NY - i) % NY] for i in range(NY)]
    sems = Sems(send_sems, recv_sems)

    barrier = pltpu.get_barrier_semaphore()

    def greet(device):
        pl.semaphore_signal(barrier, inc=1, device_id=device, device_id_type=MESH)

    for i in range(1, NZ):
        greet({"blk": at_z(zs[i])})
    for dx in range(NX):
        for dy in range(NY):
            if dx or dy:
                greet({"blk": at_xy(dx, dy)})
    from_x = lax.div(tp, HT)
    for dy in range(NY):
        for dt in range(NT):
            there = (from_x * (NZ * NY) + z * NY + ys[dy], lax.rem(tp + dt, NT))
            if dy or dt:
                greet(there)
            else:
                pl.when(from_x != xh)(functools.partial(greet, there))
    near = NZ - 1 + NX * NY - 1 + NX * NY * HT - jnp.where(from_x == xh, 1, 0)

    loads = [
        pltpu.make_async_copy(qs_hbm, qs_ref, local_sems.at[6]),
        pltpu.make_async_copy(positions_hbm, positions, local_sems.at[7]),
        pltpu.make_async_copy(k_hbm, k_ref, local_sems.at[0]),
        pltpu.make_async_copy(v_hbm, v_ref, local_sems.at[1]),
        pltpu.make_async_copy(q_hbm, q_ref, local_sems.at[2]),
        pltpu.make_async_copy(w_hbm, wt.at[xh, y], local_sems.at[5]),
    ]
    loads.append(pltpu.make_async_copy(lengths_hbm, lengths, local_sems.at[8]))
    for c in loads:
        c.start()

    def copy(src, dst, pair, device):
        return pltpu.make_async_remote_copy(
            src_ref=src, dst_ref=dst, send_sem=send_sems.at[pair], recv_sem=recv_sems.at[pair], device_id=device, device_id_type=MESH
        )

    sent = []

    def start(make):
        make().start()
        sent.append(make)

    class Queries:
        def __init__(self):
            self.p_z = [(sems.take(), sems.take()) for _ in range(1, NZ)]
            self.p_ax = (sems.take(), sems.take())
            self.p_bx = (sems.take(), sems.take())
            self.p_ay = [(sems.take(), sems.take()) for _ in range(1, NY)]
            self.p_by = [(sems.take(), sems.take()) for _ in range(1, NY)]

        def refs(self, g, *at):
            return (qa if g == 0 else qb).at[at], (pos if g == 0 else pos1).at[at]

        def send(self, g, at, pairs, device):
            for n in range(2):
                start(lambda n=n: copy(self.refs(g, *at)[n], self.refs(g, *at)[n], pairs[n], device()))

        def take(self, g, at, pairs):
            for n in range(2):
                ref = self.refs(g, *at)[n]
                copy(ref, ref, pairs[n], {"blk": at_x(other)}).wait_recv()

        def start_z(self):
            for i in range(1, NZ):
                start(lambda i=i: copy(qz.at[z], qz.at[z], self.p_z[i - 1][0], {"blk": at_z(zs[i])}))
                start(
                    lambda i=i: copy(
                        pos.at[xh, z, y], pos.at[xh, z, y], self.p_z[i - 1][1], {"blk": at_z(zs[i])}
                    )
                )

        def wait_z(self):
            for i in range(1, NZ):
                slot = qz.at[zb[i]]
                copy(slot, slot, self.p_z[i - 1][0], {"blk": at_z(zs[i])}).wait_recv()
                slot = pos.at[xh, zb[i], y]
                copy(slot, slot, self.p_z[i - 1][1], {"blk": at_z(zs[i])}).wait_recv()
            qa[xh, :, y] = qz[:, 0]
            qb[xh, :, y] = qz[:, 1]
            pos1[xh, :, y] = pos[xh, :, y]

        def start_2(self):
            self.send(0, (xh, slice(None), y), self.p_ax, lambda: {"blk": at_x(other)})
            for i in range(1, NY):
                self.send(1, (xh, slice(None), y), self.p_by[i - 1], lambda i=i: {"blk": at_y(ys[i])})

        def wait_2(self):
            self.take(0, (other, slice(None), y), self.p_ax)
            for i in range(1, NY):
                self.take(1, (xh, slice(None), yb[i]), self.p_by[i - 1])

        def start_3(self):
            for i in range(1, NY):
                self.send(0, (slice(None), slice(None), y), self.p_ay[i - 1], lambda i=i: {"blk": at_y(ys[i])})
            self.send(1, (xh,), self.p_bx, lambda: {"blk": at_x(other)})

        def wait_3y(self, i):
            self.take(0, (slice(None), slice(None), yb[i]), self.p_ay[i - 1])

        def wait_3x(self):
            self.take(1, (other,), self.p_bx)

    class Plane:
        def __init__(self, a, b):
            self.a, self.b = a, b
            self.p_ax, self.p_bx = sems.take(), sems.take()
            self.p_ay = [sems.take() for _ in range(1, NY)]
            self.p_by = [sems.take() for _ in range(1, NY)]

        def start_1(self):
            start(lambda: copy(self.a(xh, y), self.a(xh, y), self.p_ax, {"blk": at_x(other)}))
            for i in range(1, NY):
                start(lambda i=i: copy(self.b(xh, y), self.b(xh, y), self.p_by[i - 1], {"blk": at_y(ys[i])}))

        def wait_1(self):
            copy(self.a(xh, y), self.a(other, y), self.p_ax, {"blk": at_x(other)}).wait_recv()
            for i in range(1, NY):
                copy(self.b(xh, y), self.b(xh, yb[i]), self.p_by[i - 1], {"blk": at_y(ys[i])}).wait_recv()

        def start_2(self):
            for i in range(1, NY):
                start(
                    lambda i=i: copy(self.a(slice(None), y), self.a(slice(None), y), self.p_ay[i - 1], {"blk": at_y(ys[i])})
                )
            start(lambda: copy(self.b(xh, slice(None)), self.b(xh, slice(None)), self.p_bx, {"blk": at_x(other)}))

        def wait_2(self):
            for i in range(1, NY):
                copy(
                    self.a(slice(None), y), self.a(slice(None), yb[i]), self.p_ay[i - 1], {"blk": at_y(ys[i])}
                ).wait_recv()
            copy(self.b(xh, slice(None)), self.b(other, slice(None)), self.p_bx, {"blk": at_x(other)}).wait_recv()

    gather_q = Queries()
    gather_kv = Plane(lambda a, b: ak.at[a, b], lambda a, b: av.at[a, b])
    gather_w = Plane(lambda a, b: wt.at[a, b, :, 0:512], lambda a, b: wt.at[a, b, :, 512:1024])
    p_plane = [[sems.take() for _ in range(NY)] for _ in range(NX)]
    sems.used += 8
    p_kv = (sems.take(), sems.take())
    p_line = [(sems.take(), sems.take()) for _ in range(1, NZ)]
    p_att = [sems.take() for _ in range(1, NZ)]
    p_out = [sems.take() for _ in range(NX * NY * HT)]
    p_from = sems.used
    sems.used += NY * NT
    p_y0 = [(sems.take(), sems.take()) for _ in range(1, NY)]
    p_x1 = [sems.take() for _ in range(NY // NX + 1)]
    p_x0 = [(sems.take(), sems.take())]
    p_y1 = [(sems.take(), sems.take()) for _ in range(1, NY)]
    p_z01 = [(sems.take(), sems.take()) for _ in range(1, NZ)]

    loads[0].wait()
    loads[1].wait()
    q_piece = qs_ref[...].astype(F32)
    for g in range(2):
        qz[z, g] = jnp.concatenate(
            [q_piece[:, (g * 4 + h) * HEAD : (g * 4 + h + 1) * HEAD] for h in range(4)], axis=0
        ).astype(BF16)
    row = lax.broadcasted_iota(jnp.int32, (TOK, HEAD), 0)
    tile = jnp.zeros((TOK, HEAD), jnp.int32)
    for i in range(TOK):
        tile = jnp.where(row == i, positions[i], tile)
    pos[xh, z, y] = tile

    pl.semaphore_wait(barrier, near)
    gather_q.start_z()
    loads[5].wait()
    gather_w.start_1()
    loads[2].wait()
    loads[3].wait()

    share = BT // (NX * NY)

    def hand(dx, dy):
        rows = pl.ds(pl.multiple_of((dx * NY + dy) * share, share), share)
        device = {"blk": dx * (NZ * NY) + dy}
        return [
            pltpu.make_async_remote_copy(
                src_ref=src.at[rows],
                dst_ref=dst.at[dx, dy],
                send_sem=send_sems.at[p_plane[dx][dy] + n * 8],
                recv_sem=recv_sems.at[p_kv[n]],
                device_id=device,
                device_id_type=MESH,
            )
            for n, (src, dst) in enumerate(((k_ref, ak), (v_ref, av)))
        ]

    @pl.when(is_root)
    def _():
        ak[0, 0] = k_ref[0:share, :]
        av[0, 0] = v_ref[0:share, :]
        for dx in range(NX):
            for dy in range(NY):
                if dx or dy:
                    for c in hand(dx, dy):
                        c.start()

    def line(i):
        return [
            pltpu.make_async_remote_copy(
                src_ref=ref.at[xh, y],
                dst_ref=ref.at[xh, y],
                send_sem=send_sems.at[p_line[i - 1][n]],
                recv_sem=recv_sems.at[p_kv[n]],
                device_id={"blk": at_z(zs[i])},
                device_id_type=MESH,
            )
            for n, ref in enumerate((ak, av))
        ]

    def arrived():
        for c in line(1):
            c.wait_recv()

    def pass_on():
        @pl.when((z == 0) & (blk > 0))
        def _():
            arrived()

        @pl.when(z == 0)
        def _():
            for i in range(1, NZ):
                for c in line(i):
                    c.start()

    loads[6].wait()
    own_len = lengths[blk]
    anchor_len = jnp.where(is_root, 0, lengths[0])
    expand_keys(k_ref[...], v_ref[...], own_len, k_ref, kx, vx)
    loads[4].wait()

    def own_group(g, carry):
        prev = None
        for t in range(BT // TILE + 1):
            r0 = t * TILE
            here = t < BT // TILE
            if here:
                q = context_queries(q_ref, g, r0)
                m = jnp.full((ROWS, HEAD), NEG, F32)
            if prev is not None:
                acc = jnp.zeros((ROWS, 2 * HEAD), F32)
            for c in range(BT // CHUNK):
                cols = slice(c * CHUNK, (c + 1) * CHUNK)
                if here and c <= t:
                    s = dot_t(q, kx[g, cols, :])
                    if c == t:
                        i = lax.broadcasted_iota(jnp.int32, (4, TILE, CHUNK), 1).reshape(ROWS, CHUNK)
                        j = lax.broadcasted_iota(jnp.int32, (ROWS, CHUNK), 1)
                        s = jnp.where(j <= i, s, NEG)
                    s_buf[t % 2, :, cols] = s
                    m = fold_max(m, s)
                if prev is not None and c <= t - 1:
                    p = jnp.exp2(s_buf[(t - 1) % 2, :, cols] - prev).astype(BF16)
                    acc += jnp.dot(p, vx[g, cols, :], preferred_element_type=F32)
            if prev is not None:
                own_acc[g * 4 + t - 1] = acc
                own_peak[g * 4 + t - 1] = jnp.broadcast_to(prev, (ROWS, HEAD))
            if here:
                prev = jnp.max(m, axis=1, keepdims=True)
            run_hooks(own_hooks, g, t)
        return carry

    def second_step():
        gather_q.wait_z()
        gather_q.start_2()

    def run_hooks(hooks, g, t):
        for (at_g, at_t), hook in hooks.items():
            if at_t == t:
                pl.when(g == at_g)(hook)

    own_hooks = {(0, 4): second_step, (1, 2): pass_on}
    lax.fori_loop(0, 2, own_group, 0)
    gather_q.wait_2()
    gather_q.start_3()

    lane = lax.broadcasted_iota(jnp.int32, (TOK, HEAD), 1)
    dev0 = NX * NZ
    halves = NY // NX
    dev1 = NZ * NY // halves
    zpart = NZ // halves
    rows0 = dev0 * PIECE
    rows1 = dev1 * PIECE

    def scored_scores(q, limits, g, slot, count):
        rows = count * PIECE
        q = jnp.concatenate([q, q], axis=1)
        limits = jnp.concatenate([limits, limits], axis=2) - blk * BT
        m = jnp.full((rows, HEAD), NEG, F32)
        for c in range(BT // CHUNK):
            cols = slice(c * CHUNK, (c + 1) * CHUNK)
            s = dot_t(q, kx[g, cols, :]).reshape(count, 4, TOK, CHUNK)
            col = c * CHUNK + lax.broadcasted_iota(jnp.int32, (count, TOK, CHUNK), 2)
            ok = jnp.broadcast_to((col <= limits)[:, None], (count, 4, TOK, CHUNK))
            s = jnp.where(ok, s, NEG).reshape(rows, CHUNK)
            s_buf[slot, 0:rows, cols] = s
            m = fold_max(m, s)
        return jnp.max(m, axis=1, keepdims=True)

    def scored_values(peak, g, slot, count):
        rows = count * PIECE
        acc = jnp.zeros((rows, 2 * HEAD), F32)
        for c in range(BT // CHUNK):
            cols = slice(c * CHUNK, (c + 1) * CHUNK)
            p = jnp.exp2(s_buf[slot, 0:rows, cols] - peak).astype(BF16)
            acc += jnp.dot(p, vx[g, cols, :], preferred_element_type=F32)
        sums = acc[:, HEAD:]
        lse = (peak + jnp.log2(sums)).reshape(count, 4, TOK, HEAD)
        return (acc[:, :HEAD] / sums).astype(BF16), lse

    def stat_tile(lse, limits, devices, offsets):
        out = jnp.full((TOK, HEAD), NEG, F32)
        for d, offset in zip(devices, offsets):
            for h in range(4):
                out = jnp.where((lane == offset + h) & (limits[d] >= blk * BT), lse[d, h], out)
        return out

    def scored_0(i):
        yi = yb[i]
        lim0 = pos[:, :, yi].reshape(dev0, TOK, HEAD)
        peak0 = scored_scores(qa[:, :, yi].reshape(rows0, HEAD), lim0, 0, 0, dev0)
        out0, lse0 = scored_values(peak0, 0, 0, dev0)
        o0[yi] = out0.reshape(NX, NZ, PIECE, HEAD)
        st0[yi] = stat_tile(lse0, lim0, range(dev0), [(d // NZ) * 64 + (d % NZ) * 8 for d in range(dev0)])
        if i > 0:
            pairs = p_y0[NY - i - 1]
            start(lambda pair=pairs[0]: copy(o0.at[yi], r0y.at[NY - i - 1], pair, {"blk": at_y(yi)}))
            start(lambda pair=pairs[1]: copy(st0.at[yi], t0y.at[NY - i - 1], pair, {"blk": at_y(yi)}))

    def scored_1(i):
        xi = xh if i < halves else other
        z0 = (i % halves) * zpart
        lim1 = pos1[xi, z0 : z0 + zpart].reshape(dev1, TOK, HEAD)
        peak1 = scored_scores(qb[xi, z0 : z0 + zpart].reshape(rows1, HEAD), lim1, 1, 1, dev1)
        out1, lse1 = scored_values(peak1, 1, 1, dev1)
        o1[xi, z0 : z0 + zpart] = out1.reshape(zpart, NY, PIECE, HEAD)
        for yy in range(NY):
            devices = [zz * NY + yy for zz in range(zpart)]
            new = stat_tile(lse1, lim1, devices, [(z0 + zz) * 8 for zz in range(zpart)])
            st1[xi, yy] = new if i % halves == 0 else jnp.maximum(st1[xi, yy], new)

    def send_1(n):
        at = slice(n * zpart, (n + 1) * zpart)
        start(lambda: copy(o1.at[other, at], r1x.at[at], p_x1[n], {"blk": at_x(other)}))

    scored_0(0)
    for i in range(halves):
        scored_1(i)
    order = [1, 3, 2] if NY == 4 else list(range(1, NY))
    for n, i in enumerate(order):
        gather_q.wait_3y(i)
        scored_0(i)
        if n == 0:
            pl.when(z > 0)(arrived)
            gather_kv.start_1()
    gather_q.wait_3x()
    for i in range(halves, NY):
        scored_1(i)
        send_1(i - halves)
    start(lambda: copy(st1.at[other], t1x, p_x1[halves], {"blk": at_x(other)}))
    gather_kv.wait_1()
    gather_kv.start_2()

    def sums_1():
        for i in range(1, NY):
            copy(o0.at[y], r0y.at[i - 1], p_y0[i - 1][0], {"blk": at_y(ys[i])}).wait_recv()
            copy(st0.at[y], t0y.at[i - 1], p_y0[i - 1][1], {"blk": at_y(ys[i])}).wait_recv()
        ws, l0x[...] = merge([st0[y]] + [t0y[i] for i in range(NY - 1)])
        for a in range(NX):
            for b in range(NZ):
                at = a * 64 + b * 8
                total = o0[y, a, b].astype(F32) * lane_weights(ws[0], at)
                for i in range(NY - 1):
                    total += r0y[i, a, b].astype(F32) * lane_weights(ws[i + 1], at)
                o0x[a, b] = total.astype(BF16)
        start(lambda: copy(o0x.at[other], r0x, p_x0[0][0], {"blk": at_x(other)}))
        start(lambda: copy(l0x, t0x, p_x0[0][1], {"blk": at_x(other)}))
        for n in range(halves):
            at = slice(n * zpart, (n + 1) * zpart)
            copy(o1.at[xh, at], r1x.at[at], p_x1[n], {"blk": at_x(other)}).wait_recv()
        copy(st1.at[xh], t1x, p_x1[halves], {"blk": at_x(other)}).wait_recv()
        for c in range(NY):
            ws, l1y[c] = merge([st1[xh, c], t1x[c]])
            for b in range(NZ):
                total = o1[xh, b, c].astype(F32) * lane_weights(ws[0], b * 8)
                total += r1x[b, c].astype(F32) * lane_weights(ws[1], b * 8)
                o1y[c, b] = total.astype(BF16)
        for i in range(1, NY):
            start(lambda i=i: copy(o1y.at[ys[i]], r1y.at[i - 1], p_y1[i - 1][0], {"blk": at_y(ys[i])}))
            start(lambda i=i: copy(l1y.at[ys[i]], t1y.at[i - 1], p_y1[i - 1][1], {"blk": at_y(ys[i])}))

    def sums_2():
        copy(o0x.at[xh], r0x, p_x0[0][0], {"blk": at_x(other)}).wait_recv()
        copy(l0x, t0x, p_x0[0][1], {"blk": at_x(other)}).wait_recv()

        def own_x(t):
            return jnp.where(xh == 0, t, pltpu.roll(t, 64, 1))

        ws, lse = merge([own_x(l0x[...]), own_x(t0x[...])])
        lz[0] = lse
        for b in range(NZ):
            total = o0x[xh, b].astype(F32) * lane_weights(ws[0], b * 8)
            total += r0x[b].astype(F32) * lane_weights(ws[1], b * 8)
            oz[b, 0] = total.astype(BF16)
        for i in range(1, NY):
            copy(o1y.at[y], r1y.at[i - 1], p_y1[i - 1][0], {"blk": at_y(ys[i])}).wait_recv()
            copy(l1y.at[y], t1y.at[i - 1], p_y1[i - 1][1], {"blk": at_y(ys[i])}).wait_recv()
        ws, lse = merge([l1y[y]] + [t1y[i] for i in range(NY - 1)])
        lz[1] = lse
        for b in range(NZ):
            total = o1y[y, b].astype(F32) * lane_weights(ws[0], b * 8)
            for i in range(NY - 1):
                total += r1y[i, b].astype(F32) * lane_weights(ws[i + 1], b * 8)
            oz[b, 1] = total.astype(BF16)
        for i in range(1, NZ):
            start(lambda i=i: copy(oz.at[zs[i]], rz.at[i - 1], p_z01[i - 1][0], {"blk": at_z(zs[i])}))
            start(lambda i=i: copy(lz, tz.at[i - 1], p_z01[i - 1][1], {"blk": at_z(zs[i])}))

    def sums_3():
        for i in range(1, NZ):
            copy(oz.at[z], rz.at[i - 1], p_z01[i - 1][0], {"blk": at_z(zs[i])}).wait_recv()
            copy(lz, tz.at[i - 1], p_z01[i - 1][1], {"blk": at_z(zs[i])}).wait_recv()
        for g in range(2):
            ws, _ = merge([lz[g]] + [tz[i, g] for i in range(NZ - 1)])
            total = jnp.zeros((PIECE, HEAD), F32)
            for i in range(NZ):
                part = oz[z, g] if i == 0 else rz[i - 1, g]
                factor = jnp.concatenate(
                    [
                        jnp.broadcast_to(
                            jnp.sum(jnp.where(lane == z * 8 + h, ws[i], 0.0), axis=1, keepdims=True), (TOK, HEAD)
                        )
                        for h in range(4)
                    ],
                    axis=0,
                )
                total += part.astype(F32) * factor
            att[z, g] = total.astype(BF16)
        for i in range(1, NZ):
            start(lambda i=i: copy(att.at[z], att.at[z], p_att[i - 1], {"blk": at_z(zs[i])}))

    def project():
        for i in range(1, NZ):
            copy(att.at[z], att.at[zb[i]], p_att[i - 1], {"blk": at_z(zs[i])}).wait_recv()
        gather_w.wait_2()
        rows = att[...].astype(F32)
        rows = jnp.concatenate(
            [rows[:, g, h * TOK : (h + 1) * TOK].reshape(NZ * TOK, HEAD) for g in range(2) for h in range(4)], axis=1
        ).astype(BF16)
        terms = dot_t(rows, wt[...].reshape(NX * NY * 64, 1024))
        half = ZH * TOK // 2
        first = lax.broadcasted_iota(jnp.int32, (half, HEAD), 1) < 64
        for c in range(NX * NY):
            for n in range(HT):
                part = terms[n * 2 * half : (n + 1) * 2 * half, (c // 2) * HEAD : (c // 2 + 1) * HEAD]
                top, low = part[0:half], part[half : 2 * half]
                if c % 2 == 0:
                    low = pltpu.roll(low, 64, 1)
                else:
                    top = pltpu.roll(top, 64, 1)
                msg[c, n] = jnp.where(first, top, low).astype(BF16)
        for n in range(HT):
            to_t = xh * HT + n
            for dx in range(NX):
                for dy in range(NY):
                    to_x, to_y = xs[dx], ys[dy]

                    def send():
                        return pltpu.make_async_remote_copy(
                            src_ref=msg.at[to_x * NY + to_y, n],
                            dst_ref=got.at[y, tp],
                            send_sem=send_sems.at[p_out[(n * NX + dx) * NY + dy]],
                            recv_sem=recv_sems.at[p_from + y * NT + tp],
                            device_id=(to_x * (NZ * NY) + z * NY + to_y, to_t),
                            device_id_type=MESH,
                        )

                    if dx or dy:
                        send().start()
                    else:
                        pl.when(to_t != tp)(lambda: send().start())

        @pl.when(from_x == xh)
        def _():
            got[y, tp] = msg[xh * NY + y, lax.rem(tp, HT)]

    def finish():
        for sy in range(NY):
            for st in range(NT):

                def await_one():
                    pltpu.make_async_remote_copy(
                        src_ref=msg.at[0, 0],
                        dst_ref=got.at[sy, st],
                        send_sem=send_sems.at[p_out[0]],
                        recv_sem=recv_sems.at[p_from + sy * NT + st],
                        device_id=(blk, tp),
                        device_id_type=MESH,
                    ).wait_recv()

                pl.when((from_x != xh) | (sy != y) | (st != tp))(await_one)
        sums = []
        for sy in range(NY):
            total = got[sy, 0].astype(F32)
            for st in range(1, NT):
                total += got[sy, st].astype(F32)
            sums.append((total, pltpu.roll(total, 64, 1)))
        blocks = []
        for zz in range(ZH):
            for sy in range(NY):
                whole = sums[sy][zz // (ZH // 2)]
                at = (zz % (ZH // 2)) * TOK
                blocks.append(whole[at : at + TOK])
        result = jnp.concatenate(blocks, axis=0).T
        out_ref[...] = result[0:64].astype(BF16)
        for n in range(HT):
            for dx in range(NX):
                for dy in range(NY):

                    def settle():
                        pltpu.make_async_remote_copy(
                            src_ref=msg.at[0, n],
                            dst_ref=got.at[y, tp],
                            send_sem=send_sems.at[p_out[(n * NX + dx) * NY + dy]],
                            recv_sem=recv_sems.at[p_from],
                            device_id=(blk, tp),
                            device_id_type=MESH,
                        ).wait_send()

                    if dx or dy:
                        settle()
                    else:
                        pl.when(xh * HT + n != tp)(settle)

    sums_1()
    sums_2()
    gather_kv.wait_2()
    gather_w.wait_1()
    gather_w.start_2()
    expand_keys(ak[...].reshape(BT, 2 * HEAD), av[...].reshape(BT, 2 * HEAD), anchor_len, k_ref, akx, avx)
    stores = [
        pltpu.make_async_copy(out_buf.at[g], ctx_hbm.at[:, g * 512 : (g + 1) * 512], local_sems.at[3 + g])
        for g in range(2)
    ]
    anchor_hooks = {(0, 2): sums_3, (1, 0): stores[0].start, (1, 2): project}

    def anchor_group(g, carry):
        prev = None
        for t in range(BT // TILE + 1):
            r0 = t * TILE
            here = t < BT // TILE
            if here:
                q = context_queries(q_ref, g, r0)
                m = own_peak[g * 4 + t]
            if prev is not None:
                before = own_peak[g * 4 + t - 1]
                fade = jnp.exp2(before - prev)
                acc = own_acc[g * 4 + t - 1] * jnp.concatenate([fade, fade], axis=1)
            for c in range(BT // CHUNK):
                cols = slice(c * CHUNK, (c + 1) * CHUNK)
                if here:
                    s = dot_t(q, akx[g, cols, :])
                    s_buf[t % 2, :, cols] = s
                    m = fold_max(m, s)
                if prev is not None:
                    p = jnp.exp2(s_buf[(t - 1) % 2, :, cols] - prev).astype(BF16)
                    acc += jnp.dot(p, avx[g, cols, :], preferred_element_type=F32)
            if prev is not None:
                out = (acc[:, :HEAD] / acc[:, HEAD:]).astype(BF16)
                for h in range(4):
                    out_buf[g, (t - 1) * TILE : t * TILE, h * HEAD : (h + 1) * HEAD] = out[
                        h * TILE : (h + 1) * TILE
                    ]
            if here:
                prev = jnp.max(m, axis=1, keepdims=True)

            run_hooks(anchor_hooks, g, t)
        return carry

    lax.fori_loop(0, 2, anchor_group, 0)
    stores[1].start()
    finish()
    for make in sent:
        make().wait_send()

    @pl.when(is_root)
    def _():
        for dx in range(NX):
            for dy in range(NY):
                if dx or dy:
                    for c in hand(dx, dy):
                        c.wait_send()

    @pl.when(z == 0)
    def _():
        for i in range(1, NZ):
            for c in line(i):
                c.wait_send()

    for c in stores:
        c.wait()


def solution(mesh, dims=(2, 8, 4, 4), vlim=44):
    NX, NZ, NY, NT = dims
    NB = NX * NZ * NY
    vmem = pl.BlockSpec(memory_space=pltpu.VMEM)
    hbm = pl.BlockSpec(memory_space=pl.ANY)
    pieces = (NX, NZ, NY, PIECE, HEAD)
    anchor = (NX, NY, BT // (NX * NY), 2 * HEAD)
    per = NB * TOK // NT

    def local(q, k, v, lengths, q_scored, positions, weight):
        call = pl.pallas_call(
            functools.partial(kernel, dims),
            out_shape=(
                jax.ShapeDtypeStruct((BT, 1024), BF16),
                jax.ShapeDtypeStruct((64, per), BF16),
            ),
            in_specs=[pl.BlockSpec(memory_space=pltpu.HBM)] * 7,
            out_specs=(hbm, vmem),
            scratch_shapes=[
                pltpu.SMEM((NB,), jnp.int32),
                pltpu.SMEM((TOK,), jnp.int32),
                pltpu.VMEM((TOK, 1024), BF16),
                pltpu.VMEM((BT, 1024), BF16),
                pltpu.VMEM((BT, 2 * HEAD), BF16),
                pltpu.VMEM((BT, 2 * HEAD), BF16),
                pltpu.VMEM((2, BT, 512), BF16),
                pltpu.VMEM((2, BT, 2 * HEAD), BF16),
                pltpu.VMEM((2, BT, 2 * HEAD), BF16),
                pltpu.VMEM((2, BT, 2 * HEAD), BF16),
                pltpu.VMEM((2, BT, 2 * HEAD), BF16),
                pltpu.VMEM((2, ROWS, BT), F32),
                pltpu.VMEM((8, ROWS, 2 * HEAD), F32),
                pltpu.VMEM((8, ROWS, HEAD), F32),
                pltpu.VMEM((NZ, 2, PIECE, HEAD), BF16),
                pltpu.VMEM(pieces, BF16),
                pltpu.VMEM(pieces, BF16),
                pltpu.VMEM((NX, NZ, NY, TOK, HEAD), jnp.int32),
                pltpu.VMEM((NX, NZ, NY, TOK, HEAD), jnp.int32),
                pltpu.VMEM(anchor, BF16),
                pltpu.VMEM(anchor, BF16),
                pltpu.VMEM((NY, NX, NZ, PIECE, HEAD), BF16),
                pltpu.VMEM((NX, NZ, NY, PIECE, HEAD), BF16),
                pltpu.VMEM((NY, TOK, HEAD), F32),
                pltpu.VMEM((NX, NY, TOK, HEAD), F32),
                pltpu.VMEM((NY - 1, NX, NZ, PIECE, HEAD), BF16),
                pltpu.VMEM((NY - 1, TOK, HEAD), F32),
                pltpu.VMEM((NZ, NY, PIECE, HEAD), BF16),
                pltpu.VMEM((NY, TOK, HEAD), F32),
                pltpu.VMEM((NX, NZ, PIECE, HEAD), BF16),
                pltpu.VMEM((TOK, HEAD), F32),
                pltpu.VMEM((NZ, PIECE, HEAD), BF16),
                pltpu.VMEM((TOK, HEAD), F32),
                pltpu.VMEM((NY, NZ, PIECE, HEAD), BF16),
                pltpu.VMEM((NY, TOK, HEAD), F32),
                pltpu.VMEM((NY - 1, NZ, PIECE, HEAD), BF16),
                pltpu.VMEM((NY - 1, TOK, HEAD), F32),
                pltpu.VMEM((NZ, 2, PIECE, HEAD), BF16),
                pltpu.VMEM((2, TOK, HEAD), F32),
                pltpu.VMEM((NZ - 1, 2, PIECE, HEAD), BF16),
                pltpu.VMEM((NZ - 1, 2, TOK, HEAD), F32),
                pltpu.VMEM((NZ, 2, PIECE, HEAD), BF16),
                pltpu.VMEM((NX, NY, 64, 1024), BF16),
                pltpu.VMEM((NX * NY, NT // NX, NZ * NX // NT * TOK // 2, HEAD), BF16),
                pltpu.VMEM((NY, NT, NZ * NX // NT * TOK // 2, HEAD), BF16),
                pltpu.SemaphoreType.DMA((200,)),
                pltpu.SemaphoreType.DMA((200,)),
                pltpu.SemaphoreType.DMA((9,)),
            ],
            compiler_params=pltpu.CompilerParams(
                collective_id=0, has_side_effects=True, vmem_limit_bytes=vlim * 2**20
            ),
            name="star_attention",
        )
        context_out, scored_t = call(*[pltpu.with_memory_space_constraint(a, pltpu.HBM) for a in (lengths, positions, q, k, v, q_scored, weight.T)])
        return context_out, scored_t.T

    in_specs = (P("blk", "tp"), P("blk", "tp"), P("blk", "tp"), P(), P("blk", "tp"), P("blk"), P("tp", "blk"))
    out_specs = (P("blk", "tp"), P("tp", "blk"))
    return jax.shard_map(local, mesh=mesh, in_specs=in_specs, out_specs=out_specs, check_vma=False)
```

```python
import functools
import math

import jax
import jax.numpy as jnp
from jax import lax
from jax.experimental import pallas as pl
from jax.experimental.pallas import tpu as pltpu
from jax.sharding import PartitionSpec as P

BT = 1024
HEAD = 128
TOK = 8
PIECE = 4 * TOK
LOG2_SCALE = math.log2(math.e) / math.sqrt(HEAD)
NEG = -1e30
CHUNK = 256
TILE = 256
ROWS = 4 * TILE
MESH = pl.DeviceIdType.MESH
F32 = jnp.float32
BF16 = jnp.bfloat16


def dot_t(a, b):
    return lax.dot_general(a, b, (((1,), (1,)), ((), ())), preferred_element_type=F32)


def expand_keys(keys, values, live_len, filler_ref, kx, vx):
    live = lax.broadcasted_iota(jnp.int32, (BT, HEAD), 0) < live_len
    for g in range(2):
        cols = slice(g * HEAD, (g + 1) * HEAD)
        scaled = jnp.where(live, keys[:, cols].astype(F32), filler_ref[0:16, cols].astype(F32)[0:1]) * LOG2_SCALE
        high = scaled.astype(BF16)
        kx[g, :, 0:HEAD] = high
        kx[g, :, HEAD : 2 * HEAD] = (scaled - high.astype(F32)).astype(BF16)
        vx[g, :, 0:HEAD] = jnp.where(live, values[:, cols].astype(F32), 0.0).astype(BF16)
        vx[g, :, HEAD : 2 * HEAD] = jnp.where(live, 1.0, 0.0).astype(BF16)


def fold_max(m, s):
    for j in range(0, s.shape[1], HEAD):
        m = jnp.maximum(m, s[:, j : j + HEAD])
    return m


def context_queries(q_ref, g, r0):
    parts = [
        q_ref[r0 : r0 + TILE, pl.ds(pl.multiple_of(g * 512 + h * HEAD, HEAD), HEAD)] for h in range(4)
    ]
    q = jnp.concatenate(parts, axis=0)
    return jnp.concatenate([q, q], axis=1)


class Sems:
    def __init__(self, send, recv):
        self.send, self.recv, self.used = send, recv, 0

    def take(self):
        i = self.used
        self.used += 1
        return i


def merge(lses):
    best = functools.reduce(jnp.maximum, lses)
    terms = [jnp.exp2(l - best) for l in lses]
    total = functools.reduce(jnp.add, terms)
    return [t / total for t in terms], best + jnp.log2(total)


def lane_weights(w, lane):
    return jnp.concatenate(
        [jnp.broadcast_to(w[:, lane + h : lane + h + 1], (TOK, HEAD)) for h in range(4)], axis=0
    )


def kernel(
    dims,
    lengths_hbm,
    positions_hbm,
    q_hbm,
    k_hbm,
    v_hbm,
    qs_hbm,
    w_hbm,
    ctx_hbm,
    out_ref,
    lengths,
    positions,
    qs_ref,
    q_ref,
    k_ref,
    v_ref,
    out_buf,
    kx,
    vx,
    akx,
    avx,
    s_buf,
    own_acc,
    own_peak,
    qz,
    qa,
    qb,
    pos,
    pos1,
    ak,
    av,
    o0,
    o1,
    st0,
    st1,
    r0y,
    t0y,
    r1x,
    t1x,
    o0x,
    l0x,
    r0x,
    t0x,
    o1y,
    l1y,
    r1y,
    t1y,
    oz,
    lz,
    rz,
    tz,
    att,
    wt,
    msg,
    got,
    send_sems,
    recv_sems,
    local_sems,
):
    NX, NZ, NY, NT = dims
    NB = NX * NZ * NY
    blk = lax.axis_index("blk")
    tp = lax.axis_index("tp")
    xh = lax.div(blk, NZ * NY)
    z = lax.rem(lax.div(blk, NY), NZ)
    y = lax.rem(blk, NY)
    is_root = blk == 0
    HT = NT // NX
    ZH = NZ // HT
    other = NX - 1 - xh

    def at_x(v):
        return v * (NZ * NY) + z * NY + y

    def at_z(v):
        return xh * (NZ * NY) + v * NY + y

    def at_y(v):
        return xh * (NZ * NY) + z * NY + v

    def at_xy(dx, dy):
        return xs[dx] * (NZ * NY) + z * NY + ys[dy]

    xs = [xh, NX - 1 - xh]
    zs = [z] + [lax.rem(z + i, NZ) for i in range(1, NZ)]
    ys = [y] + [lax.rem(y + i, NY) for i in range(1, NY)]
    zb = [zs[(NZ - i) % NZ] for i in range(NZ)]
    yb = [ys[(NY - i) % NY] for i in range(NY)]
    sems = Sems(send_sems, recv_sems)

    barrier = pltpu.get_barrier_semaphore()

    def greet(device):
        pl.semaphore_signal(barrier, inc=1, device_id=device, device_id_type=MESH)

    for i in range(1, NZ):
        greet({"blk": at_z(zs[i])})
    for dx in range(NX):
        for dy in range(NY):
            if dx or dy:
                greet({"blk": at_xy(dx, dy)})
    from_x = lax.div(tp, HT)
    for dy in range(NY):
        for dt in range(NT):
            there = (from_x * (NZ * NY) + z * NY + ys[dy], lax.rem(tp + dt, NT))
            if dy or dt:
                greet(there)
            else:
                pl.when(from_x != xh)(functools.partial(greet, there))
    near = NZ - 1 + NX * NY - 1 + NX * NY * HT - jnp.where(from_x == xh, 1, 0)

    loads = [
        pltpu.make_async_copy(qs_hbm, qs_ref, local_sems.at[6]),
        pltpu.make_async_copy(positions_hbm, positions, local_sems.at[7]),
        pltpu.make_async_copy(k_hbm, k_ref, local_sems.at[0]),
        pltpu.make_async_copy(v_hbm, v_ref, local_sems.at[1]),
        pltpu.make_async_copy(q_hbm, q_ref, local_sems.at[2]),
        pltpu.make_async_copy(w_hbm, wt.at[xh, y], local_sems.at[5]),
    ]
    loads.append(pltpu.make_async_copy(lengths_hbm, lengths, local_sems.at[8]))
    for c in loads:
        c.start()

    def copy(src, dst, pair, device):
        return pltpu.make_async_remote_copy(
            src_ref=src, dst_ref=dst, send_sem=send_sems.at[pair], recv_sem=recv_sems.at[pair], device_id=device, device_id_type=MESH
        )

    def copy_to(src, dst, send, recv, device):
        return pltpu.make_async_remote_copy(
            src_ref=src,
            dst_ref=dst,
            send_sem=send_sems.at[send],
            recv_sem=recv_sems.at[recv],
            device_id=device,
            device_id_type=MESH,
        )

    sent = []

    def start(make):
        make().start()
        sent.append(make)

    class Queries:
        def __init__(self):
            self.p_z = [(sems.take(), sems.take()) for _ in range(1, NZ)]
            self.p_ax = (sems.take(), sems.take())
            self.p_bx = (sems.take(), sems.take())
            self.p_ay = [(sems.take(), sems.take()) for _ in range(1, NY)]
            self.p_by = [(sems.take(), sems.take()) for _ in range(1, NY)]

        def refs(self, g, *at):
            return (qa if g == 0 else qb).at[at], (pos if g == 0 else pos1).at[at]

        def send(self, g, at, pairs, device):
            for n in range(2):
                start(lambda n=n: copy(self.refs(g, *at)[n], self.refs(g, *at)[n], pairs[n], device()))

        def take(self, g, at, pairs):
            for n in range(2):
                ref = self.refs(g, *at)[n]
                copy(ref, ref, pairs[n], {"blk": at_x(other)}).wait_recv()

        def start_z(self):
            for i in range(1, NZ):
                start(lambda i=i: copy(qz.at[z], qz.at[z], self.p_z[i - 1][0], {"blk": at_z(zs[i])}))
                start(
                    lambda i=i: copy(
                        pos.at[xh, z, y], pos.at[xh, z, y], self.p_z[i - 1][1], {"blk": at_z(zs[i])}
                    )
                )

        def wait_z(self):
            for i in range(1, NZ):
                slot = qz.at[zb[i]]
                copy(slot, slot, self.p_z[i - 1][0], {"blk": at_z(zs[i])}).wait_recv()
                slot = pos.at[xh, zb[i], y]
                copy(slot, slot, self.p_z[i - 1][1], {"blk": at_z(zs[i])}).wait_recv()
            qa[xh, :, y] = qz[:, 0]
            qb[xh, :, y] = qz[:, 1]
            pos1[xh, :, y] = pos[xh, :, y]

        def start_2(self):
            self.send(0, (xh, slice(None), y), self.p_ax, lambda: {"blk": at_x(other)})
            for i in range(1, NY):
                self.send(1, (xh, slice(None), y), self.p_by[i - 1], lambda i=i: {"blk": at_y(ys[i])})

        def wait_2(self):
            self.take(0, (other, slice(None), y), self.p_ax)
            for i in range(1, NY):
                self.take(1, (xh, slice(None), yb[i]), self.p_by[i - 1])

        def start_3(self):
            for i in range(1, NY):
                self.send(0, (slice(None), slice(None), y), self.p_ay[i - 1], lambda i=i: {"blk": at_y(ys[i])})
            self.send(1, (xh,), self.p_bx, lambda: {"blk": at_x(other)})

        def wait_3y(self, i):
            self.take(0, (slice(None), slice(None), yb[i]), self.p_ay[i - 1])

        def wait_3x(self):
            self.take(1, (other,), self.p_bx)

    class Plane:
        def __init__(self, a, b):
            self.a, self.b = a, b
            self.p_ax, self.p_bx = sems.take(), sems.take()
            self.p_ay = [sems.take() for _ in range(1, NY)]
            self.p_by = [sems.take() for _ in range(1, NY)]

        def start_1(self):
            start(lambda: copy(self.a(xh, y), self.a(xh, y), self.p_ax, {"blk": at_x(other)}))
            for i in range(1, NY):
                start(lambda i=i: copy(self.b(xh, y), self.b(xh, y), self.p_by[i - 1], {"blk": at_y(ys[i])}))

        def wait_1(self):
            copy(self.a(xh, y), self.a(other, y), self.p_ax, {"blk": at_x(other)}).wait_recv()
            for i in range(1, NY):
                copy(self.b(xh, y), self.b(xh, yb[i]), self.p_by[i - 1], {"blk": at_y(ys[i])}).wait_recv()

        def start_2(self):
            for i in range(1, NY):
                start(
                    lambda i=i: copy(self.a(slice(None), y), self.a(slice(None), y), self.p_ay[i - 1], {"blk": at_y(ys[i])})
                )
            start(lambda: copy(self.b(xh, slice(None)), self.b(xh, slice(None)), self.p_bx, {"blk": at_x(other)}))

        def wait_2(self):
            for i in range(1, NY):
                copy(
                    self.a(slice(None), y), self.a(slice(None), yb[i]), self.p_ay[i - 1], {"blk": at_y(ys[i])}
                ).wait_recv()
            copy(self.b(xh, slice(None)), self.b(other, slice(None)), self.p_bx, {"blk": at_x(other)}).wait_recv()

    gather_q = Queries()
    gather_k = Plane(lambda a, b: ak.at[a, b, :, 0:HEAD], lambda a, b: ak.at[a, b, :, HEAD : 2 * HEAD])
    gather_w = Plane(lambda a, b: wt.at[a, b, :, 0:512], lambda a, b: wt.at[a, b, :, 512:1024])
    p_hand_k = [[sems.take() for _ in range(NY)] for _ in range(NX)]
    p_pass_v = [[sems.take() for _ in range(NY)] for _ in range(NX)]
    p_hand_v = [sems.take() for _ in range(NZ)]
    p_pass_k = [sems.take() for _ in range(NZ)]
    p_line_v = [sems.take() for _ in range(NZ)]
    p_k, p_v = sems.take(), sems.take()
    p_att = [sems.take() for _ in range(1, NZ)]
    p_out = [sems.take() for _ in range(NX * NY * HT)]
    p_from = sems.used
    sems.used += NY * NT
    p_y0 = [(sems.take(), sems.take()) for _ in range(1, NY)]
    p_x1 = [sems.take() for _ in range(NY // NX + 1)]
    p_x0 = [(sems.take(), sems.take())]
    p_y1 = [(sems.take(), sems.take()) for _ in range(1, NY)]
    p_z01 = [(sems.take(), sems.take()) for _ in range(1, NZ)]

    loads[0].wait()
    loads[1].wait()
    q_piece = qs_ref[...].astype(F32)
    for g in range(2):
        qz[z, g] = jnp.concatenate(
            [q_piece[:, (g * 4 + h) * HEAD : (g * 4 + h + 1) * HEAD] for h in range(4)], axis=0
        ).astype(BF16)
    row = lax.broadcasted_iota(jnp.int32, (1, HEAD), 1)
    line_of = jnp.zeros((1, HEAD), jnp.int32)
    for i in range(TOK):
        line_of = jnp.where(row == i, positions[i], line_of)
    pos[xh, z, y] = line_of

    pl.semaphore_wait(barrier, near)
    gather_q.start_z()
    loads[5].wait()
    gather_w.start_1()
    loads[2].wait()
    loads[3].wait()

    share_k = BT // (NX * NY)
    share_v = BT // NZ

    def hand_k(dx, dy):
        rows = pl.ds((dx * NY + dy) * share_k, share_k)
        return copy_to(k_ref.at[rows], ak.at[dx, dy], p_hand_k[dx][dy], p_k, {"blk": dx * (NZ * NY) + dy})

    def hand_v(i):
        return copy_to(v_ref.at[pl.ds(i * share_v, share_v)], av.at[i], p_hand_v[i], p_v, {"blk": i * NY})

    def pass_k(i):
        return copy_to(ak.at[xh, y], ak.at[xh, y], p_pass_k[i], p_k, {"blk": at_z(zs[i])})

    def pass_v(dx, dy):
        return copy_to(av.at[z], av.at[z], p_pass_v[dx][dy], p_v, {"blk": at_xy(dx, dy)})

    def line_v(i):
        return copy(av.at[z], av.at[z], p_line_v[i], {"blk": at_z(zs[i])})

    plane = [(dx, dy) for dx in range(NX) for dy in range(NY) if dx or dy]
    is_head = (xh == 0) & (y == 0)

    @pl.when(is_root)
    def _():
        ak[0, 0] = k_ref[0:share_k, :]
        av[0] = v_ref[0:share_v, :]
        for dx, dy in plane:
            hand_k(dx, dy).start()
        for i in range(1, NZ):
            hand_v(i).start()

    def pass_on_k():
        @pl.when((z == 0) & (blk > 0))
        def _():
            pass_k(1).wait_recv()

        @pl.when(z == 0)
        def _():
            for i in range(1, NZ):
                pass_k(i).start()

    def pass_on_v():
        @pl.when(is_head & (z > 0))
        def _():
            pass_v(0, 1).wait_recv()

        @pl.when(is_head)
        def _():
            for dx, dy in plane:
                pass_v(dx, dy).start()

    def gather_v():
        @pl.when(jnp.logical_not(is_head))
        def _():
            pass_v(0, 1).wait_recv()

        for i in range(1, NZ):
            line_v(i).start()

    def settle_kv():
        @pl.when(is_root)
        def _():
            for dx, dy in plane:
                hand_k(dx, dy).wait_send()
            for i in range(1, NZ):
                hand_v(i).wait_send()

        @pl.when(z == 0)
        def _():
            for i in range(1, NZ):
                pass_k(i).wait_send()

        @pl.when(is_head)
        def _():
            for dx, dy in plane:
                pass_v(dx, dy).wait_send()

        for i in range(1, NZ):
            line_v(i).wait_send()

    loads[6].wait()
    own_len = lengths[blk]
    anchor_len = jnp.where(is_root, 0, lengths[0])
    expand_keys(k_ref[...], v_ref[...], own_len, k_ref, kx, vx)
    loads[4].wait()

    def own_group(g, carry):
        prev = None
        for t in range(BT // TILE + 1):
            r0 = t * TILE
            here = t < BT // TILE
            if here:
                q = context_queries(q_ref, g, r0)
                m = jnp.full((ROWS, HEAD), NEG, F32)
            if prev is not None:
                acc = jnp.zeros((ROWS, 2 * HEAD), F32)
            for c in range(BT // CHUNK):
                cols = slice(c * CHUNK, (c + 1) * CHUNK)
                if here and c <= t:
                    s = dot_t(q, kx[g, cols, :])
                    if c == t:
                        i = lax.broadcasted_iota(jnp.int32, (4, TILE, CHUNK), 1).reshape(ROWS, CHUNK)
                        j = lax.broadcasted_iota(jnp.int32, (ROWS, CHUNK), 1)
                        s = jnp.where(j <= i, s, NEG)
                    s_buf[t % 2, :, cols] = s
                    m = fold_max(m, s)
                if prev is not None and c <= t - 1:
                    p = jnp.exp2(s_buf[(t - 1) % 2, :, cols] - prev).astype(BF16)
                    acc += jnp.dot(p, vx[g, cols, :], preferred_element_type=F32)
            if prev is not None:
                own_acc[g * 4 + t - 1] = acc
                own_peak[g * 4 + t - 1] = jnp.broadcast_to(prev, (ROWS, HEAD))
            if here:
                prev = jnp.max(m, axis=1, keepdims=True)
            run_hooks(own_hooks, g, t)
        return carry

    def second_step():
        gather_q.wait_z()
        gather_q.start_2()

    def run_hooks(hooks, g, t):
        for (at_g, at_t), hook in hooks.items():
            if at_t == t:
                pl.when(g == at_g)(hook)

    own_hooks = {(0, 4): second_step, (1, 2): pass_on_k, (1, 4): pass_on_v}
    lax.fori_loop(0, 2, own_group, 0)
    gather_q.wait_2()
    gather_q.start_3()

    lane = lax.broadcasted_iota(jnp.int32, (TOK, HEAD), 1)
    dev0 = NX * NZ
    halves = NY // NX
    dev1 = NZ * NY // halves
    zpart = NZ // halves
    rows0 = dev0 * PIECE
    rows1 = dev1 * PIECE

    def limits_of(rows, count):
        pick = lax.broadcasted_iota(jnp.int32, (count, TOK, HEAD), 1) == lax.broadcasted_iota(
            jnp.int32, (count, TOK, HEAD), 2
        )
        spread = jnp.where(pick, jnp.broadcast_to(rows.astype(F32), (count, TOK, HEAD)), 0.0)
        spread = jnp.broadcast_to(jnp.sum(spread, axis=2, keepdims=True), (count, TOK, HEAD))
        return spread.astype(jnp.int32) - blk * BT

    def scored_scores(q, limits, g, slot, count):
        rows = count * PIECE
        q = jnp.concatenate([q, q], axis=1)
        limits = jnp.concatenate([limits, limits], axis=2)
        m = jnp.full((rows, HEAD), NEG, F32)
        for c in range(BT // CHUNK):
            cols = slice(c * CHUNK, (c + 1) * CHUNK)
            s = dot_t(q, kx[g, cols, :]).reshape(count, 4, TOK, CHUNK)
            col = c * CHUNK + lax.broadcasted_iota(jnp.int32, (count, TOK, CHUNK), 2)
            ok = jnp.broadcast_to((col <= limits)[:, None], (count, 4, TOK, CHUNK))
            s = jnp.where(ok, s, NEG).reshape(rows, CHUNK)
            s_buf[slot, 0:rows, cols] = s
            m = fold_max(m, s)
        return jnp.max(m, axis=1, keepdims=True)

    def scored_values(peak, g, slot, count):
        rows = count * PIECE
        acc = jnp.zeros((rows, 2 * HEAD), F32)
        for c in range(BT // CHUNK):
            cols = slice(c * CHUNK, (c + 1) * CHUNK)
            p = jnp.exp2(s_buf[slot, 0:rows, cols] - peak).astype(BF16)
            acc += jnp.dot(p, vx[g, cols, :], preferred_element_type=F32)
        sums = acc[:, HEAD:]
        lse = (peak + jnp.log2(sums)).reshape(count, 4, TOK, HEAD)
        return (acc[:, :HEAD] / sums).astype(BF16), lse

    def stat_tile(lse, limits, devices, offsets):
        out = jnp.full((TOK, HEAD), NEG, F32)
        for d, offset in zip(devices, offsets):
            for h in range(4):
                out = jnp.where((lane == offset + h) & (limits[d] >= 0), lse[d, h], out)
        return out

    def scored_0(i):
        yi = yb[i]
        lim0 = limits_of(pos[:, :, yi].reshape(dev0, 1, HEAD), dev0)
        peak0 = scored_scores(qa[:, :, yi].reshape(rows0, HEAD), lim0, 0, 0, dev0)
        out0, lse0 = scored_values(peak0, 0, 0, dev0)
        o0[yi] = out0.reshape(NX, NZ, PIECE, HEAD)
        st0[yi] = stat_tile(lse0, lim0, range(dev0), [(d // NZ) * 64 + (d % NZ) * 8 for d in range(dev0)])
        if i > 0:
            pairs = p_y0[NY - i - 1]
            start(lambda pair=pairs[0]: copy(o0.at[yi], r0y.at[NY - i - 1], pair, {"blk": at_y(yi)}))
            start(lambda pair=pairs[1]: copy(st0.at[yi], t0y.at[NY - i - 1], pair, {"blk": at_y(yi)}))

    def scored_1(i):
        xi = xh if i < halves else other
        z0 = (i % halves) * zpart
        lim1 = limits_of(pos1[xi, z0 : z0 + zpart].reshape(dev1, 1, HEAD), dev1)
        peak1 = scored_scores(qb[xi, z0 : z0 + zpart].reshape(rows1, HEAD), lim1, 1, 1, dev1)
        out1, lse1 = scored_values(peak1, 1, 1, dev1)
        o1[xi, z0 : z0 + zpart] = out1.reshape(zpart, NY, PIECE, HEAD)
        for yy in range(NY):
            devices = [zz * NY + yy for zz in range(zpart)]
            new = stat_tile(lse1, lim1, devices, [(z0 + zz) * 8 for zz in range(zpart)])
            st1[xi, yy] = new if i % halves == 0 else jnp.maximum(st1[xi, yy], new)

    def send_1(n):
        at = slice(n * zpart, (n + 1) * zpart)
        start(lambda: copy(o1.at[other, at], r1x.at[at], p_x1[n], {"blk": at_x(other)}))

    scored_0(0)
    for i in range(halves):
        scored_1(i)
    pl.when(z > 0)(lambda: pass_k(1).wait_recv())
    gather_k.start_1()
    gather_v()
    order = [1, 3, 2] if NY == 4 else list(range(1, NY))
    for n, i in enumerate(order):
        gather_q.wait_3y(i)
        scored_0(i)
    gather_q.wait_3x()
    for i in range(halves, NY):
        scored_1(i)
        send_1(i - halves)
    start(lambda: copy(st1.at[other], t1x, p_x1[halves], {"blk": at_x(other)}))
    gather_k.wait_1()
    gather_k.start_2()

    def sums_1():
        for i in range(1, NY):
            copy(o0.at[y], r0y.at[i - 1], p_y0[i - 1][0], {"blk": at_y(ys[i])}).wait_recv()
            copy(st0.at[y], t0y.at[i - 1], p_y0[i - 1][1], {"blk": at_y(ys[i])}).wait_recv()
        ws, l0x[...] = merge([st0[y]] + [t0y[i] for i in range(NY - 1)])
        for a in range(NX):
            for b in range(NZ):
                at = a * 64 + b * 8
                total = o0[y, a, b].astype(F32) * lane_weights(ws[0], at)
                for i in range(NY - 1):
                    total += r0y[i, a, b].astype(F32) * lane_weights(ws[i + 1], at)
                o0x[a, b] = total.astype(BF16)
        start(lambda: copy(o0x.at[other], r0x, p_x0[0][0], {"blk": at_x(other)}))
        start(lambda: copy(l0x, t0x, p_x0[0][1], {"blk": at_x(other)}))
        for n in range(halves):
            at = slice(n * zpart, (n + 1) * zpart)
            copy(o1.at[xh, at], r1x.at[at], p_x1[n], {"blk": at_x(other)}).wait_recv()
        copy(st1.at[xh], t1x, p_x1[halves], {"blk": at_x(other)}).wait_recv()
        for c in range(NY):
            ws, l1y[c] = merge([st1[xh, c], t1x[c]])
            for b in range(NZ):
                total = o1[xh, b, c].astype(F32) * lane_weights(ws[0], b * 8)
                total += r1x[b, c].astype(F32) * lane_weights(ws[1], b * 8)
                o1y[c, b] = total.astype(BF16)
        for i in range(1, NY):
            start(lambda i=i: copy(o1y.at[ys[i]], r1y.at[i - 1], p_y1[i - 1][0], {"blk": at_y(ys[i])}))
            start(lambda i=i: copy(l1y.at[ys[i]], t1y.at[i - 1], p_y1[i - 1][1], {"blk": at_y(ys[i])}))

    def sums_2():
        copy(o0x.at[xh], r0x, p_x0[0][0], {"blk": at_x(other)}).wait_recv()
        copy(l0x, t0x, p_x0[0][1], {"blk": at_x(other)}).wait_recv()

        def own_x(t):
            return jnp.where(xh == 0, t, pltpu.roll(t, 64, 1))

        ws, lse = merge([own_x(l0x[...]), own_x(t0x[...])])
        lse0 = lse
        for b in range(NZ):
            total = o0x[xh, b].astype(F32) * lane_weights(ws[0], b * 8)
            total += r0x[b].astype(F32) * lane_weights(ws[1], b * 8)
            oz[b, 0] = total.astype(BF16)
        for i in range(1, NY):
            copy(o1y.at[y], r1y.at[i - 1], p_y1[i - 1][0], {"blk": at_y(ys[i])}).wait_recv()
            copy(l1y.at[y], t1y.at[i - 1], p_y1[i - 1][1], {"blk": at_y(ys[i])}).wait_recv()
        ws, lse = merge([l1y[y]] + [t1y[i] for i in range(NY - 1)])
        lz[...] = jnp.where(lax.rem(lane, 8) < 4, lse0, pltpu.roll(lse, 4, 1))
        for b in range(NZ):
            total = o1y[y, b].astype(F32) * lane_weights(ws[0], b * 8)
            for i in range(NY - 1):
                total += r1y[i, b].astype(F32) * lane_weights(ws[i + 1], b * 8)
            oz[b, 1] = total.astype(BF16)
        for i in range(1, NZ):
            start(lambda i=i: copy(oz.at[zs[i]], rz.at[i - 1], p_z01[i - 1][0], {"blk": at_z(zs[i])}))
            start(lambda i=i: copy(lz, tz.at[i - 1], p_z01[i - 1][1], {"blk": at_z(zs[i])}))

    def sums_3():
        for i in range(1, NZ):
            copy(oz.at[z], rz.at[i - 1], p_z01[i - 1][0], {"blk": at_z(zs[i])}).wait_recv()
            copy(lz, tz.at[i - 1], p_z01[i - 1][1], {"blk": at_z(zs[i])}).wait_recv()
        ws, _ = merge([lz[...]] + [tz[i] for i in range(NZ - 1)])
        for g in range(2):
            total = jnp.zeros((PIECE, HEAD), F32)
            for i in range(NZ):
                part = oz[z, g] if i == 0 else rz[i - 1, g]
                factor = jnp.concatenate(
                    [
                        jnp.broadcast_to(
                            jnp.sum(jnp.where(lane == z * 8 + g * 4 + h, ws[i], 0.0), axis=1, keepdims=True), (TOK, HEAD)
                        )
                        for h in range(4)
                    ],
                    axis=0,
                )
                total += part.astype(F32) * factor
            att[z, g] = total.astype(BF16)
        for i in range(1, NZ):
            start(lambda i=i: copy(att.at[z], att.at[z], p_att[i - 1], {"blk": at_z(zs[i])}))

    def project():
        for i in range(1, NZ):
            copy(att.at[z], att.at[zb[i]], p_att[i - 1], {"blk": at_z(zs[i])}).wait_recv()
        gather_w.wait_2()
        rows = att[...].astype(F32)
        rows = jnp.concatenate(
            [rows[:, g, h * TOK : (h + 1) * TOK].reshape(NZ * TOK, HEAD) for g in range(2) for h in range(4)], axis=1
        ).astype(BF16)
        terms = dot_t(rows, wt[...].reshape(NX * NY * 64, 1024))
        half = ZH * TOK // 2
        first = lax.broadcasted_iota(jnp.int32, (half, HEAD), 1) < 64
        for c in range(NX * NY):
            for n in range(HT):
                part = terms[n * 2 * half : (n + 1) * 2 * half, (c // 2) * HEAD : (c // 2 + 1) * HEAD]
                top, low = part[0:half], part[half : 2 * half]
                if c % 2 == 0:
                    low = pltpu.roll(low, 64, 1)
                else:
                    top = pltpu.roll(top, 64, 1)
                msg[c, n] = jnp.where(first, top, low).astype(BF16)
        for n in range(HT):
            to_t = xh * HT + n
            for dx in range(NX):
                for dy in range(NY):
                    to_x, to_y = xs[dx], ys[dy]

                    def send():
                        return pltpu.make_async_remote_copy(
                            src_ref=msg.at[to_x * NY + to_y, n],
                            dst_ref=got.at[y, tp],
                            send_sem=send_sems.at[p_out[(n * NX + dx) * NY + dy]],
                            recv_sem=recv_sems.at[p_from + y * NT + tp],
                            device_id=(to_x * (NZ * NY) + z * NY + to_y, to_t),
                            device_id_type=MESH,
                        )

                    if dx or dy:
                        send().start()
                    else:
                        pl.when(to_t != tp)(lambda: send().start())

        @pl.when(from_x == xh)
        def _():
            got[y, tp] = msg[xh * NY + y, lax.rem(tp, HT)]

    def finish():
        for sy in range(NY):
            for st in range(NT):

                def await_one():
                    pltpu.make_async_remote_copy(
                        src_ref=msg.at[0, 0],
                        dst_ref=got.at[sy, st],
                        send_sem=send_sems.at[p_out[0]],
                        recv_sem=recv_sems.at[p_from + sy * NT + st],
                        device_id=(blk, tp),
                        device_id_type=MESH,
                    ).wait_recv()

                pl.when((from_x != xh) | (sy != y) | (st != tp))(await_one)
        sums = []
        for sy in range(NY):
            total = got[sy, 0].astype(F32)
            for st in range(1, NT):
                total += got[sy, st].astype(F32)
            sums.append((total, pltpu.roll(total, 64, 1)))
        blocks = []
        for zz in range(ZH):
            for sy in range(NY):
                whole = sums[sy][zz // (ZH // 2)]
                at = (zz % (ZH // 2)) * TOK
                blocks.append(whole[at : at + TOK])
        result = jnp.concatenate(blocks, axis=0).T
        out_ref[...] = result[0:64].astype(BF16)
        for n in range(HT):
            for dx in range(NX):
                for dy in range(NY):

                    def settle():
                        pltpu.make_async_remote_copy(
                            src_ref=msg.at[0, n],
                            dst_ref=got.at[y, tp],
                            send_sem=send_sems.at[p_out[(n * NX + dx) * NY + dy]],
                            recv_sem=recv_sems.at[p_from],
                            device_id=(blk, tp),
                            device_id_type=MESH,
                        ).wait_send()

                    if dx or dy:
                        settle()
                    else:
                        pl.when(xh * HT + n != tp)(settle)

    def weights_2():
        sums_2()
        gather_w.wait_1()
        gather_w.start_2()

    def attended():
        sums_3()
        stores[0].start()

    sums_1()
    gather_k.wait_2()
    for i in range(1, NZ):
        copy(av.at[z], av.at[zb[i]], p_line_v[i], {"blk": at_z(zs[i])}).wait_recv()
    expand_keys(ak[...].reshape(BT, 2 * HEAD), av[...].reshape(BT, 2 * HEAD), anchor_len, k_ref, akx, avx)
    stores = [
        pltpu.make_async_copy(out_buf.at[g], ctx_hbm.at[:, g * 512 : (g + 1) * 512], local_sems.at[3 + g])
        for g in range(2)
    ]
    anchor_hooks = {(0, 2): weights_2, (1, 0): attended, (1, 3): project}

    def anchor_group(g, carry):
        prev = None
        for t in range(BT // TILE + 1):
            r0 = t * TILE
            here = t < BT // TILE
            if here:
                q = context_queries(q_ref, g, r0)
                m = own_peak[g * 4 + t]
            if prev is not None:
                before = own_peak[g * 4 + t - 1]
                fade = jnp.exp2(before - prev)
                acc = own_acc[g * 4 + t - 1] * jnp.concatenate([fade, fade], axis=1)
            for c in range(BT // CHUNK):
                cols = slice(c * CHUNK, (c + 1) * CHUNK)
                if here:
                    s = dot_t(q, akx[g, cols, :])
                    s_buf[t % 2, :, cols] = s
                    m = fold_max(m, s)
                if prev is not None:
                    p = jnp.exp2(s_buf[(t - 1) % 2, :, cols] - prev).astype(BF16)
                    acc += jnp.dot(p, avx[g, cols, :], preferred_element_type=F32)
            if prev is not None:
                out = (acc[:, :HEAD] / acc[:, HEAD:]).astype(BF16)
                for h in range(4):
                    out_buf[g, (t - 1) * TILE : t * TILE, h * HEAD : (h + 1) * HEAD] = out[
                        h * TILE : (h + 1) * TILE
                    ]
            if here:
                prev = jnp.max(m, axis=1, keepdims=True)

            run_hooks(anchor_hooks, g, t)
        return carry

    lax.fori_loop(0, 2, anchor_group, 0)
    stores[1].start()
    finish()
    for make in sent:
        make().wait_send()

    settle_kv()
    for c in stores:
        c.wait()


def solution(mesh, dims=(2, 8, 4, 4), vlim=44):
    NX, NZ, NY, NT = dims
    NB = NX * NZ * NY
    vmem = pl.BlockSpec(memory_space=pltpu.VMEM)
    hbm = pl.BlockSpec(memory_space=pl.ANY)
    pieces = (NX, NZ, NY, PIECE, HEAD)
    anchor = (NX, NY, BT // (NX * NY), 2 * HEAD)
    per = NB * TOK // NT

    def local(q, k, v, lengths, q_scored, positions, weight):
        call = pl.pallas_call(
            functools.partial(kernel, dims),
            out_shape=(
                jax.ShapeDtypeStruct((BT, 1024), BF16),
                jax.ShapeDtypeStruct((64, per), BF16),
            ),
            in_specs=[pl.BlockSpec(memory_space=pltpu.HBM)] * 7,
            out_specs=(hbm, vmem),
            scratch_shapes=[
                pltpu.SMEM((NB,), jnp.int32),
                pltpu.SMEM((TOK,), jnp.int32),
                pltpu.VMEM((TOK, 1024), BF16),
                pltpu.VMEM((BT, 1024), BF16),
                pltpu.VMEM((BT, 2 * HEAD), BF16),
                pltpu.VMEM((BT, 2 * HEAD), BF16),
                pltpu.VMEM((2, BT, 512), BF16),
                pltpu.VMEM((2, BT, 2 * HEAD), BF16),
                pltpu.VMEM((2, BT, 2 * HEAD), BF16),
                pltpu.VMEM((2, BT, 2 * HEAD), BF16),
                pltpu.VMEM((2, BT, 2 * HEAD), BF16),
                pltpu.VMEM((2, ROWS, BT), F32),
                pltpu.VMEM((8, ROWS, 2 * HEAD), F32),
                pltpu.VMEM((8, ROWS, HEAD), F32),
                pltpu.VMEM((NZ, 2, PIECE, HEAD), BF16),
                pltpu.VMEM(pieces, BF16),
                pltpu.VMEM(pieces, BF16),
                pltpu.VMEM((NX, NZ, NY, 1, HEAD), jnp.int32),
                pltpu.VMEM((NX, NZ, NY, 1, HEAD), jnp.int32),
                pltpu.VMEM(anchor, BF16),
                pltpu.VMEM((NZ, BT // NZ, 2 * HEAD), BF16),
                pltpu.VMEM((NY, NX, NZ, PIECE, HEAD), BF16),
                pltpu.VMEM((NX, NZ, NY, PIECE, HEAD), BF16),
                pltpu.VMEM((NY, TOK, HEAD), F32),
                pltpu.VMEM((NX, NY, TOK, HEAD), F32),
                pltpu.VMEM((NY - 1, NX, NZ, PIECE, HEAD), BF16),
                pltpu.VMEM((NY - 1, TOK, HEAD), F32),
                pltpu.VMEM((NZ, NY, PIECE, HEAD), BF16),
                pltpu.VMEM((NY, TOK, HEAD), F32),
                pltpu.VMEM((NX, NZ, PIECE, HEAD), BF16),
                pltpu.VMEM((TOK, HEAD), F32),
                pltpu.VMEM((NZ, PIECE, HEAD), BF16),
                pltpu.VMEM((TOK, HEAD), F32),
                pltpu.VMEM((NY, NZ, PIECE, HEAD), BF16),
                pltpu.VMEM((NY, TOK, HEAD), F32),
                pltpu.VMEM((NY - 1, NZ, PIECE, HEAD), BF16),
                pltpu.VMEM((NY - 1, TOK, HEAD), F32),
                pltpu.VMEM((NZ, 2, PIECE, HEAD), BF16),
                pltpu.VMEM((TOK, HEAD), F32),
                pltpu.VMEM((NZ - 1, 2, PIECE, HEAD), BF16),
                pltpu.VMEM((NZ - 1, TOK, HEAD), F32),
                pltpu.VMEM((NZ, 2, PIECE, HEAD), BF16),
                pltpu.VMEM((NX, NY, 64, 1024), BF16),
                pltpu.VMEM((NX * NY, NT // NX, NZ * NX // NT * TOK // 2, HEAD), BF16),
                pltpu.VMEM((NY, NT, NZ * NX // NT * TOK // 2, HEAD), BF16),
                pltpu.SemaphoreType.DMA((240,)),
                pltpu.SemaphoreType.DMA((240,)),
                pltpu.SemaphoreType.DMA((9,)),
            ],
            compiler_params=pltpu.CompilerParams(
                collective_id=0, has_side_effects=True, vmem_limit_bytes=vlim * 2**20
            ),
            name="star_attention",
        )
        arrays = (lengths, positions, q, k, v, q_scored, weight.T)
        context_out, scored_t = call(*[pltpu.with_memory_space_constraint(a, pltpu.HBM) for a in arrays])
        return context_out, scored_t.T

    in_specs = (P("blk", "tp"), P("blk", "tp"), P("blk", "tp"), P(), P("blk", "tp"), P("blk"), P("tp", "blk"))
    out_specs = (P("blk", "tp"), P("tp", "blk"))
    return jax.shard_map(local, mesh=mesh, in_specs=in_specs, out_specs=out_specs, check_vma=False)
```

```python
import functools
import math

import jax
import jax.numpy as jnp
from jax import lax
from jax.experimental import pallas as pl
from jax.experimental.pallas import tpu as pltpu
from jax.sharding import PartitionSpec as P

BT = 1024
HEAD = 128
TOK = 8
PIECE = 4 * TOK
LOG2_SCALE = math.log2(math.e) / math.sqrt(HEAD)
NEG = -1e30
CHUNK = 256
TILE = 256
ROWS = 4 * TILE
MESH = pl.DeviceIdType.MESH
F32 = jnp.float32
BF16 = jnp.bfloat16


def dot_t(a, b):
    return lax.dot_general(a, b, (((1,), (1,)), ((), ())), preferred_element_type=F32)


def expand_keys(keys, values, live_len, filler_ref, kx, vx):
    live = lax.broadcasted_iota(jnp.int32, (BT, HEAD), 0) < live_len
    for g in range(2):
        cols = slice(g * HEAD, (g + 1) * HEAD)
        scaled = jnp.where(live, keys[:, cols].astype(F32), filler_ref[0:16, cols].astype(F32)[0:1]) * LOG2_SCALE
        high = scaled.astype(BF16)
        kx[g, :, 0:HEAD] = high
        kx[g, :, HEAD : 2 * HEAD] = (scaled - high.astype(F32)).astype(BF16)
        vx[g, :, 0:HEAD] = jnp.where(live, values[:, cols].astype(F32), 0.0).astype(BF16)
        vx[g, :, HEAD : 2 * HEAD] = jnp.where(live, 1.0, 0.0).astype(BF16)


def fold_max(m, s):
    for j in range(0, s.shape[1], HEAD):
        m = jnp.maximum(m, s[:, j : j + HEAD])
    return m


def context_queries(q_ref, g, r0):
    parts = [
        q_ref[r0 : r0 + TILE, pl.ds(pl.multiple_of(g * 512 + h * HEAD, HEAD), HEAD)] for h in range(4)
    ]
    q = jnp.concatenate(parts, axis=0)
    return jnp.concatenate([q, q], axis=1)


class Sems:
    def __init__(self, send, recv):
        self.send, self.recv, self.used = send, recv, 0

    def take(self):
        i = self.used
        self.used += 1
        return i


def merge(lses):
    best = functools.reduce(jnp.maximum, lses)
    terms = [jnp.exp2(l - best) for l in lses]
    total = functools.reduce(jnp.add, terms)
    return [t / total for t in terms], best + jnp.log2(total)


def lane_weights(w, lane):
    return jnp.concatenate(
        [jnp.broadcast_to(w[:, lane + h : lane + h + 1], (TOK, HEAD)) for h in range(4)], axis=0
    )


def kernel(
    dims,
    lengths_hbm,
    positions_hbm,
    q_hbm,
    k_hbm,
    v_hbm,
    qs_hbm,
    w_hbm,
    ctx_hbm,
    out_ref,
    lengths,
    positions,
    qs_ref,
    q_ref,
    k_ref,
    v_ref,
    out_buf,
    kx,
    vx,
    akx,
    avx,
    s_buf,
    own_acc,
    own_peak,
    qz,
    qa,
    qb,
    pos,
    pos1,
    ak,
    av,
    o0,
    o1,
    st0,
    st1,
    r0,
    t0,
    r1,
    t1,
    oz,
    lz,
    rz,
    tz,
    att,
    wt,
    msg,
    got,
    send_sems,
    recv_sems,
    local_sems,
):
    NX, NZ, NY, NT = dims
    NB = NX * NZ * NY
    blk = lax.axis_index("blk")
    tp = lax.axis_index("tp")
    xh = lax.div(blk, NZ * NY)
    z = lax.rem(lax.div(blk, NY), NZ)
    y = lax.rem(blk, NY)
    is_root = blk == 0
    HT = NT // NX
    ZH = NZ // HT
    other = NX - 1 - xh

    def at_x(v):
        return v * (NZ * NY) + z * NY + y

    def at_z(v):
        return xh * (NZ * NY) + v * NY + y

    def at_y(v):
        return xh * (NZ * NY) + z * NY + v

    def at_xy(dx, dy):
        return xs[dx] * (NZ * NY) + z * NY + ys[dy]

    xs = [xh, NX - 1 - xh]
    zs = [z] + [lax.rem(z + i, NZ) for i in range(1, NZ)]
    ys = [y] + [lax.rem(y + i, NY) for i in range(1, NY)]
    zb = [zs[(NZ - i) % NZ] for i in range(NZ)]
    yb = [ys[(NY - i) % NY] for i in range(NY)]
    sems = Sems(send_sems, recv_sems)

    barrier = pltpu.get_barrier_semaphore()

    def greet(device):
        pl.semaphore_signal(barrier, inc=1, device_id=device, device_id_type=MESH)

    for i in range(1, NZ):
        greet({"blk": at_z(zs[i])})
    for dx in range(NX):
        for dy in range(NY):
            if dx or dy:
                greet({"blk": at_xy(dx, dy)})
    from_x = lax.div(tp, HT)
    for dy in range(NY):
        for dt in range(NT):
            there = (from_x * (NZ * NY) + z * NY + ys[dy], lax.rem(tp + dt, NT))
            if dy or dt:
                greet(there)
            else:
                pl.when(from_x != xh)(functools.partial(greet, there))
    near = NZ - 1 + NX * NY - 1 + NX * NY * HT - jnp.where(from_x == xh, 1, 0)

    loads = [
        pltpu.make_async_copy(qs_hbm, qs_ref, local_sems.at[6]),
        pltpu.make_async_copy(positions_hbm, positions, local_sems.at[7]),
        pltpu.make_async_copy(k_hbm, k_ref, local_sems.at[0]),
        pltpu.make_async_copy(v_hbm, v_ref, local_sems.at[1]),
        pltpu.make_async_copy(q_hbm, q_ref, local_sems.at[2]),
        pltpu.make_async_copy(w_hbm, wt.at[xh, y], local_sems.at[5]),
    ]
    loads.append(pltpu.make_async_copy(lengths_hbm, lengths, local_sems.at[8]))
    for c in loads:
        c.start()

    def copy(src, dst, pair, device):
        return pltpu.make_async_remote_copy(
            src_ref=src, dst_ref=dst, send_sem=send_sems.at[pair], recv_sem=recv_sems.at[pair], device_id=device, device_id_type=MESH
        )

    def copy_to(src, dst, send, recv, device):
        return pltpu.make_async_remote_copy(
            src_ref=src,
            dst_ref=dst,
            send_sem=send_sems.at[send],
            recv_sem=recv_sems.at[recv],
            device_id=device,
            device_id_type=MESH,
        )

    sent = []

    def start(make):
        make().start()
        sent.append(make)

    class Queries:
        def __init__(self):
            self.p_z = [(sems.take(), sems.take()) for _ in range(1, NZ)]
            self.p_ax = (sems.take(), sems.take())
            self.p_bx = (sems.take(), sems.take())
            self.p_ay = [(sems.take(), sems.take()) for _ in range(1, NY)]
            self.p_by = [(sems.take(), sems.take()) for _ in range(1, NY)]

        def refs(self, g, *at):
            return (qa if g == 0 else qb).at[at], (pos if g == 0 else pos1).at[at]

        def send(self, g, at, pairs, device):
            for n in range(2):
                start(lambda n=n: copy(self.refs(g, *at)[n], self.refs(g, *at)[n], pairs[n], device()))

        def take(self, g, at, pairs):
            for n in range(2):
                ref = self.refs(g, *at)[n]
                copy(ref, ref, pairs[n], {"blk": at_x(other)}).wait_recv()

        def start_z(self):
            for i in range(1, NZ):
                start(lambda i=i: copy(qz.at[z], qz.at[z], self.p_z[i - 1][0], {"blk": at_z(zs[i])}))
                start(
                    lambda i=i: copy(
                        pos.at[xh, z, y], pos.at[xh, z, y], self.p_z[i - 1][1], {"blk": at_z(zs[i])}
                    )
                )

        def wait_z(self):
            for i in range(1, NZ):
                slot = qz.at[zb[i]]
                copy(slot, slot, self.p_z[i - 1][0], {"blk": at_z(zs[i])}).wait_recv()
                slot = pos.at[xh, zb[i], y]
                copy(slot, slot, self.p_z[i - 1][1], {"blk": at_z(zs[i])}).wait_recv()
            qa[xh, :, y] = qz[:, 0]
            qb[xh, :, y] = qz[:, 1]
            pos1[xh, :, y] = pos[xh, :, y]

        def start_2(self):
            self.send(0, (xh, slice(None), y), self.p_ax, lambda: {"blk": at_x(other)})
            for i in range(1, NY):
                self.send(1, (xh, slice(None), y), self.p_by[i - 1], lambda i=i: {"blk": at_y(ys[i])})

        def wait_2(self):
            self.take(0, (other, slice(None), y), self.p_ax)
            for i in range(1, NY):
                self.take(1, (xh, slice(None), yb[i]), self.p_by[i - 1])

        def start_3(self):
            for i in range(1, NY):
                self.send(0, (slice(None), slice(None), y), self.p_ay[i - 1], lambda i=i: {"blk": at_y(ys[i])})
            self.send(1, (xh,), self.p_bx, lambda: {"blk": at_x(other)})

        def wait_3y(self, i):
            self.take(0, (slice(None), slice(None), yb[i]), self.p_ay[i - 1])

        def wait_3x(self):
            self.take(1, (other,), self.p_bx)

    class Plane:
        def __init__(self, a, b):
            self.a, self.b = a, b
            self.p_ax, self.p_bx = sems.take(), sems.take()
            self.p_ay = [sems.take() for _ in range(1, NY)]
            self.p_by = [sems.take() for _ in range(1, NY)]

        def start_1(self):
            start(lambda: copy(self.a(xh, y), self.a(xh, y), self.p_ax, {"blk": at_x(other)}))
            for i in range(1, NY):
                start(lambda i=i: copy(self.b(xh, y), self.b(xh, y), self.p_by[i - 1], {"blk": at_y(ys[i])}))

        def wait_1(self):
            copy(self.a(xh, y), self.a(other, y), self.p_ax, {"blk": at_x(other)}).wait_recv()
            for i in range(1, NY):
                copy(self.b(xh, y), self.b(xh, yb[i]), self.p_by[i - 1], {"blk": at_y(ys[i])}).wait_recv()

        def start_2(self):
            for i in range(1, NY):
                start(
                    lambda i=i: copy(self.a(slice(None), y), self.a(slice(None), y), self.p_ay[i - 1], {"blk": at_y(ys[i])})
                )
            start(lambda: copy(self.b(xh, slice(None)), self.b(xh, slice(None)), self.p_bx, {"blk": at_x(other)}))

        def wait_2(self):
            for i in range(1, NY):
                copy(
                    self.a(slice(None), y), self.a(slice(None), yb[i]), self.p_ay[i - 1], {"blk": at_y(ys[i])}
                ).wait_recv()
            copy(self.b(xh, slice(None)), self.b(other, slice(None)), self.p_bx, {"blk": at_x(other)}).wait_recv()

    gather_q = Queries()
    gather_k = Plane(lambda a, b: ak.at[a, b, :, 0:HEAD], lambda a, b: ak.at[a, b, :, HEAD : 2 * HEAD])
    gather_w = Plane(lambda a, b: wt.at[a, b, :, 0:512], lambda a, b: wt.at[a, b, :, 512:1024])
    p_hand_k = [[sems.take() for _ in range(NY)] for _ in range(NX)]
    p_pass_v = [[sems.take() for _ in range(NY)] for _ in range(NX)]
    p_hand_v = [sems.take() for _ in range(NZ)]
    p_pass_k = [sems.take() for _ in range(NZ)]
    p_line_v = [sems.take() for _ in range(NZ)]
    p_k, p_v = sems.take(), sems.take()
    p_att = [sems.take() for _ in range(1, NZ)]
    p_out = [sems.take() for _ in range(NX * NY * HT)]
    p_from = sems.used
    sems.used += NY * NT
    p_sum = [[sems.take() for _ in range(4)] for _ in range(NX * NY)]
    p_z01 = [(sems.take(), sems.take()) for _ in range(1, NZ)]

    loads[0].wait()
    loads[1].wait()
    q_piece = qs_ref[...].astype(F32)
    for g in range(2):
        qz[z, g] = jnp.concatenate(
            [q_piece[:, (g * 4 + h) * HEAD : (g * 4 + h + 1) * HEAD] for h in range(4)], axis=0
        ).astype(BF16)
    row = lax.broadcasted_iota(jnp.int32, (1, HEAD), 1)
    line_of = jnp.zeros((1, HEAD), jnp.int32)
    for i in range(TOK):
        line_of = jnp.where(row == i, positions[i], line_of)
    pos[xh, z, y] = line_of

    pl.semaphore_wait(barrier, near)
    gather_q.start_z()
    loads[5].wait()
    gather_w.start_1()
    loads[2].wait()
    loads[3].wait()

    share_k = BT // (NX * NY)
    share_v = BT // NZ

    def hand_k(dx, dy):
        rows = pl.ds((dx * NY + dy) * share_k, share_k)
        return copy_to(k_ref.at[rows], ak.at[dx, dy], p_hand_k[dx][dy], p_k, {"blk": dx * (NZ * NY) + dy})

    def hand_v(i):
        return copy_to(v_ref.at[pl.ds(i * share_v, share_v)], av.at[i], p_hand_v[i], p_v, {"blk": i * NY})

    def pass_k(i):
        return copy_to(ak.at[xh, y], ak.at[xh, y], p_pass_k[i], p_k, {"blk": at_z(zs[i])})

    def pass_v(dx, dy):
        return copy_to(av.at[z], av.at[z], p_pass_v[dx][dy], p_v, {"blk": at_xy(dx, dy)})

    def line_v(i):
        return copy(av.at[z], av.at[z], p_line_v[i], {"blk": at_z(zs[i])})

    plane = [(dx, dy) for dx in range(NX) for dy in range(NY) if dx or dy]
    is_head = (xh == 0) & (y == 0)

    @pl.when(is_root)
    def _():
        ak[0, 0] = k_ref[0:share_k, :]
        av[0] = v_ref[0:share_v, :]
        for dx, dy in plane:
            hand_k(dx, dy).start()
        for i in range(1, NZ):
            hand_v(i).start()

    def pass_on_k():
        @pl.when((z == 0) & (blk > 0))
        def _():
            pass_k(1).wait_recv()

        @pl.when(z == 0)
        def _():
            for i in range(1, NZ):
                pass_k(i).start()

    def pass_on_v():
        @pl.when(is_head & (z > 0))
        def _():
            pass_v(0, 1).wait_recv()

        @pl.when(is_head)
        def _():
            for dx, dy in plane:
                pass_v(dx, dy).start()

    def gather_v():
        @pl.when(jnp.logical_not(is_head))
        def _():
            pass_v(0, 1).wait_recv()

        for i in range(1, NZ):
            line_v(i).start()

    def settle_kv():
        @pl.when(is_root)
        def _():
            for dx, dy in plane:
                hand_k(dx, dy).wait_send()
            for i in range(1, NZ):
                hand_v(i).wait_send()

        @pl.when(z == 0)
        def _():
            for i in range(1, NZ):
                pass_k(i).wait_send()

        @pl.when(is_head)
        def _():
            for dx, dy in plane:
                pass_v(dx, dy).wait_send()

        for i in range(1, NZ):
            line_v(i).wait_send()

    loads[6].wait()
    own_len = lengths[blk]
    anchor_len = jnp.where(is_root, 0, lengths[0])
    expand_keys(k_ref[...], v_ref[...], own_len, k_ref, kx, vx)
    loads[4].wait()

    def own_group(g, carry):
        prev = None
        for t in range(BT // TILE + 1):
            r0 = t * TILE
            here = t < BT // TILE
            if here:
                q = context_queries(q_ref, g, r0)
                m = jnp.full((ROWS, HEAD), NEG, F32)
            if prev is not None:
                acc = jnp.zeros((ROWS, 2 * HEAD), F32)
            for c in range(BT // CHUNK):
                cols = slice(c * CHUNK, (c + 1) * CHUNK)
                if here and c <= t:
                    s = dot_t(q, kx[g, cols, :])
                    if c == t:
                        i = lax.broadcasted_iota(jnp.int32, (4, TILE, CHUNK), 1).reshape(ROWS, CHUNK)
                        j = lax.broadcasted_iota(jnp.int32, (ROWS, CHUNK), 1)
                        s = jnp.where(j <= i, s, NEG)
                    s_buf[t % 2, :, cols] = s
                    m = fold_max(m, s)
                if prev is not None and c <= t - 1:
                    p = jnp.exp2(s_buf[(t - 1) % 2, :, cols] - prev).astype(BF16)
                    acc += jnp.dot(p, vx[g, cols, :], preferred_element_type=F32)
            if prev is not None:
                own_acc[g * 4 + t - 1] = acc
                own_peak[g * 4 + t - 1] = jnp.broadcast_to(prev, (ROWS, HEAD))
            if here:
                prev = jnp.max(m, axis=1, keepdims=True)
            run_hooks(own_hooks, g, t)
        return carry

    def second_step():
        gather_q.wait_z()
        gather_q.start_2()

    def run_hooks(hooks, g, t):
        for (at_g, at_t), hook in hooks.items():
            if at_t == t:
                pl.when(g == at_g)(hook)

    own_hooks = {(0, 4): second_step, (1, 2): pass_on_k, (1, 4): pass_on_v}
    lax.fori_loop(0, 2, own_group, 0)
    gather_q.wait_2()
    gather_q.start_3()

    lane = lax.broadcasted_iota(jnp.int32, (TOK, HEAD), 1)
    dev0 = NX * NZ
    halves = NY // NX
    dev1 = NZ * NY // halves
    zpart = NZ // halves
    rows0 = dev0 * PIECE
    rows1 = dev1 * PIECE

    def limits_of(rows, count):
        pick = lax.broadcasted_iota(jnp.int32, (count, TOK, HEAD), 1) == lax.broadcasted_iota(
            jnp.int32, (count, TOK, HEAD), 2
        )
        spread = jnp.where(pick, jnp.broadcast_to(rows.astype(F32), (count, TOK, HEAD)), 0.0)
        spread = jnp.broadcast_to(jnp.sum(spread, axis=2, keepdims=True), (count, TOK, HEAD))
        return spread.astype(jnp.int32) - blk * BT

    def scored_scores(q, limits, g, slot, count):
        rows = count * PIECE
        q = jnp.concatenate([q, q], axis=1)
        limits = jnp.concatenate([limits, limits], axis=2)
        m = jnp.full((rows, HEAD), NEG, F32)
        for c in range(BT // CHUNK):
            cols = slice(c * CHUNK, (c + 1) * CHUNK)
            s = dot_t(q, kx[g, cols, :]).reshape(count, 4, TOK, CHUNK)
            col = c * CHUNK + lax.broadcasted_iota(jnp.int32, (count, TOK, CHUNK), 2)
            ok = jnp.broadcast_to((col <= limits)[:, None], (count, 4, TOK, CHUNK))
            s = jnp.where(ok, s, NEG).reshape(rows, CHUNK)
            s_buf[slot, 0:rows, cols] = s
            m = fold_max(m, s)
        return jnp.max(m, axis=1, keepdims=True)

    def scored_values(peak, g, slot, count):
        rows = count * PIECE
        acc = jnp.zeros((rows, 2 * HEAD), F32)
        for c in range(BT // CHUNK):
            cols = slice(c * CHUNK, (c + 1) * CHUNK)
            p = jnp.exp2(s_buf[slot, 0:rows, cols] - peak).astype(BF16)
            acc += jnp.dot(p, vx[g, cols, :], preferred_element_type=F32)
        sums = acc[:, HEAD:]
        lse = (peak + jnp.log2(sums)).reshape(count, 4, TOK, HEAD)
        return (acc[:, :HEAD] / sums).astype(BF16), lse

    def stat_tile(lse, limits, devices, offsets):
        out = jnp.full((TOK, HEAD), NEG, F32)
        for d, offset in zip(devices, offsets):
            for h in range(4):
                out = jnp.where((lane == offset + h) & (limits[d] >= 0), lse[d, h], out)
        return out

    def scored_0(i):
        yi = yb[i]
        lim0 = limits_of(pos[:, :, yi].reshape(dev0, 1, HEAD), dev0)
        peak0 = scored_scores(qa[:, :, yi].reshape(rows0, HEAD), lim0, 0, 0, dev0)
        out0, lse0 = scored_values(peak0, 0, 0, dev0)
        o0[yi] = out0.reshape(NX, NZ, PIECE, HEAD)
        st0[yi] = stat_tile(lse0, lim0, range(dev0), [(d // NZ) * 64 + (d % NZ) * 8 for d in range(dev0)])
    def scored_1(i):
        xi = xh if i < halves else other
        z0 = (i % halves) * zpart
        lim1 = limits_of(pos1[xi, z0 : z0 + zpart].reshape(dev1, 1, HEAD), dev1)
        peak1 = scored_scores(qb[xi, z0 : z0 + zpart].reshape(rows1, HEAD), lim1, 1, 1, dev1)
        out1, lse1 = scored_values(peak1, 1, 1, dev1)
        o1[xi, z0 : z0 + zpart] = out1.reshape(zpart, NY, PIECE, HEAD)
        for yy in range(NY):
            devices = [zz * NY + yy for zz in range(zpart)]
            new = stat_tile(lse1, lim1, devices, [(z0 + zz) * 8 for zz in range(zpart)])
            st1[xi, yy] = new if i % halves == 0 else jnp.maximum(st1[xi, yy], new)

    def send_sum(g, dx, dy):
        k = dx * NY + dy
        if g == 0:
            parts = lambda: ((o0.at[ys[dy], xs[dx]], r0.at[k]), (st0.at[ys[dy]], t0.at[k]))
        else:
            parts = lambda: ((o1.at[xs[dx], :, ys[dy]], r1.at[k]), (st1.at[xs[dx], ys[dy]], t1.at[k]))
        for n in range(2):
            start(lambda n=n: copy(*parts()[n], p_sum[k][2 * g + n], {"blk": at_xy(dx, dy)}))

    scored_0(0)
    for i in range(halves):
        scored_1(i)
    pl.when(z > 0)(lambda: pass_k(1).wait_recv())
    gather_k.start_1()
    gather_v()
    order = [1, 3, 2] if NY == 4 else list(range(1, NY))
    for n, i in enumerate(order):
        gather_q.wait_3y(i)
        scored_0(i)
        for dx in range(NX):
            send_sum(0, dx, NY - i)
    gather_q.wait_3x()
    send_sum(0, 1, 0)
    for dy in range(1, NY):
        send_sum(1, 0, dy)
    for i in range(halves, NY):
        scored_1(i)
    for dy in range(NY):
        send_sum(1, 1, dy)
    gather_k.wait_1()
    gather_k.start_2()

    def sums_12():
        for dx, dy in plane:
            k = dx * NY + dy
            pairs = (
                (o0.at[y, xh], r0.at[k]),
                (st0.at[y], t0.at[k]),
                (o1.at[xh, :, y], r1.at[k]),
                (st1.at[xh, y], t1.at[k]),
            )
            for n, (src, dst) in enumerate(pairs):
                copy(src, dst, p_sum[k][n], {"blk": at_x(other)}).wait_recv()
        slots = [dx * NY + dy for dx, dy in plane]

        def own_x(t):
            return jnp.where(xh == 0, t, pltpu.roll(t, 64, 1))

        ws0, lse0 = merge([own_x(t) for t in [st0[y]] + [t0[k] for k in slots]])
        ws1, lse1 = merge([st1[xh, y]] + [t1[k] for k in slots])
        lz[...] = jnp.where(lax.rem(lane, 8) < 4, lse0, pltpu.roll(lse1, 4, 1))
        for b in range(NZ):
            for g, ws, mine, theirs in ((0, ws0, o0[y, xh, b], r0), (1, ws1, o1[xh, b, y], r1)):
                total = mine.astype(F32) * lane_weights(ws[0], b * 8)
                for n, k in enumerate(slots):
                    total += theirs[k, b].astype(F32) * lane_weights(ws[n + 1], b * 8)
                oz[b, g] = total.astype(BF16)
        for i in range(1, NZ):
            start(lambda i=i: copy(oz.at[zs[i]], rz.at[i - 1], p_z01[i - 1][0], {"blk": at_z(zs[i])}))
            start(lambda i=i: copy(lz, tz.at[i - 1], p_z01[i - 1][1], {"blk": at_z(zs[i])}))

    def sums_3():
        for i in range(1, NZ):
            copy(oz.at[z], rz.at[i - 1], p_z01[i - 1][0], {"blk": at_z(zs[i])}).wait_recv()
            copy(lz, tz.at[i - 1], p_z01[i - 1][1], {"blk": at_z(zs[i])}).wait_recv()
        ws, _ = merge([lz[...]] + [tz[i] for i in range(NZ - 1)])
        for g in range(2):
            total = jnp.zeros((PIECE, HEAD), F32)
            for i in range(NZ):
                part = oz[z, g] if i == 0 else rz[i - 1, g]
                factor = jnp.concatenate(
                    [
                        jnp.broadcast_to(
                            jnp.sum(jnp.where(lane == z * 8 + g * 4 + h, ws[i], 0.0), axis=1, keepdims=True), (TOK, HEAD)
                        )
                        for h in range(4)
                    ],
                    axis=0,
                )
                total += part.astype(F32) * factor
            att[z, g] = total.astype(BF16)
        for i in range(1, NZ):
            start(lambda i=i: copy(att.at[z], att.at[z], p_att[i - 1], {"blk": at_z(zs[i])}))

    def project():
        for i in range(1, NZ):
            copy(att.at[z], att.at[zb[i]], p_att[i - 1], {"blk": at_z(zs[i])}).wait_recv()
        gather_w.wait_2()
        rows = att[...].astype(F32)
        rows = jnp.concatenate(
            [rows[:, g, h * TOK : (h + 1) * TOK].reshape(NZ * TOK, HEAD) for g in range(2) for h in range(4)], axis=1
        ).astype(BF16)
        terms = dot_t(rows, wt[...].reshape(NX * NY * 64, 1024))
        half = ZH * TOK // 2
        first = lax.broadcasted_iota(jnp.int32, (half, HEAD), 1) < 64
        for c in range(NX * NY):
            for n in range(HT):
                part = terms[n * 2 * half : (n + 1) * 2 * half, (c // 2) * HEAD : (c // 2 + 1) * HEAD]
                top, low = part[0:half], part[half : 2 * half]
                if c % 2 == 0:
                    low = pltpu.roll(low, 64, 1)
                else:
                    top = pltpu.roll(top, 64, 1)
                msg[c, n] = jnp.where(first, top, low).astype(BF16)
        for n in range(HT):
            to_t = xh * HT + n
            for dx in range(NX):
                for dy in range(NY):
                    to_x, to_y = xs[dx], ys[dy]

                    def send():
                        return pltpu.make_async_remote_copy(
                            src_ref=msg.at[to_x * NY + to_y, n],
                            dst_ref=got.at[y, tp],
                            send_sem=send_sems.at[p_out[(n * NX + dx) * NY + dy]],
                            recv_sem=recv_sems.at[p_from + y * NT + tp],
                            device_id=(to_x * (NZ * NY) + z * NY + to_y, to_t),
                            device_id_type=MESH,
                        )

                    if dx or dy:
                        send().start()
                    else:
                        pl.when(to_t != tp)(lambda: send().start())

        @pl.when(from_x == xh)
        def _():
            got[y, tp] = msg[xh * NY + y, lax.rem(tp, HT)]

    def finish():
        for sy in range(NY):
            for st in range(NT):

                def await_one():
                    pltpu.make_async_remote_copy(
                        src_ref=msg.at[0, 0],
                        dst_ref=got.at[sy, st],
                        send_sem=send_sems.at[p_out[0]],
                        recv_sem=recv_sems.at[p_from + sy * NT + st],
                        device_id=(blk, tp),
                        device_id_type=MESH,
                    ).wait_recv()

                pl.when((from_x != xh) | (sy != y) | (st != tp))(await_one)
        sums = []
        for sy in range(NY):
            total = got[sy, 0].astype(F32)
            for st in range(1, NT):
                total += got[sy, st].astype(F32)
            sums.append((total, pltpu.roll(total, 64, 1)))
        blocks = []
        for zz in range(ZH):
            for sy in range(NY):
                whole = sums[sy][zz // (ZH // 2)]
                at = (zz % (ZH // 2)) * TOK
                blocks.append(whole[at : at + TOK])
        result = jnp.concatenate(blocks, axis=0).T
        out_ref[...] = result[0:64].astype(BF16)
        for n in range(HT):
            for dx in range(NX):
                for dy in range(NY):

                    def settle():
                        pltpu.make_async_remote_copy(
                            src_ref=msg.at[0, n],
                            dst_ref=got.at[y, tp],
                            send_sem=send_sems.at[p_out[(n * NX + dx) * NY + dy]],
                            recv_sem=recv_sems.at[p_from],
                            device_id=(blk, tp),
                            device_id_type=MESH,
                        ).wait_send()

                    if dx or dy:
                        settle()
                    else:
                        pl.when(xh * HT + n != tp)(settle)

    def weights_2():
        sums_12()
        gather_w.wait_1()
        gather_w.start_2()

    weights_2()
    gather_k.wait_2()
    for i in range(1, NZ):
        copy(av.at[z], av.at[zb[i]], p_line_v[i], {"blk": at_z(zs[i])}).wait_recv()
    expand_keys(ak[...].reshape(BT, 2 * HEAD), av[...].reshape(BT, 2 * HEAD), anchor_len, k_ref, akx, avx)
    stores = [
        pltpu.make_async_copy(out_buf.at[g], ctx_hbm.at[:, g * 512 : (g + 1) * 512], local_sems.at[3 + g])
        for g in range(2)
    ]
    anchor_hooks = {(0, 2): sums_3, (1, 0): stores[0].start, (1, 1): project}

    def anchor_group(g, carry):
        prev = None
        for t in range(BT // TILE + 1):
            r0 = t * TILE
            here = t < BT // TILE
            if here:
                q = context_queries(q_ref, g, r0)
                m = own_peak[g * 4 + t]
            if prev is not None:
                before = own_peak[g * 4 + t - 1]
                fade = jnp.exp2(before - prev)
                acc = own_acc[g * 4 + t - 1] * jnp.concatenate([fade, fade], axis=1)
            for c in range(BT // CHUNK):
                cols = slice(c * CHUNK, (c + 1) * CHUNK)
                if here:
                    s = dot_t(q, akx[g, cols, :])
                    s_buf[t % 2, :, cols] = s
                    m = fold_max(m, s)
                if prev is not None:
                    p = jnp.exp2(s_buf[(t - 1) % 2, :, cols] - prev).astype(BF16)
                    acc += jnp.dot(p, avx[g, cols, :], preferred_element_type=F32)
            if prev is not None:
                out = (acc[:, :HEAD] / acc[:, HEAD:]).astype(BF16)
                for h in range(4):
                    out_buf[g, (t - 1) * TILE : t * TILE, h * HEAD : (h + 1) * HEAD] = out[
                        h * TILE : (h + 1) * TILE
                    ]
            if here:
                prev = jnp.max(m, axis=1, keepdims=True)

            run_hooks(anchor_hooks, g, t)
        return carry

    lax.fori_loop(0, 2, anchor_group, 0)
    stores[1].start()
    finish()
    for make in sent:
        make().wait_send()

    settle_kv()
    for c in stores:
        c.wait()


def solution(mesh, dims=(2, 8, 4, 4), vlim=44):
    NX, NZ, NY, NT = dims
    NB = NX * NZ * NY
    vmem = pl.BlockSpec(memory_space=pltpu.VMEM)
    hbm = pl.BlockSpec(memory_space=pl.ANY)
    pieces = (NX, NZ, NY, PIECE, HEAD)
    anchor = (NX, NY, BT // (NX * NY), 2 * HEAD)
    per = NB * TOK // NT

    def local(q, k, v, lengths, q_scored, positions, weight):
        call = pl.pallas_call(
            functools.partial(kernel, dims),
            out_shape=(
                jax.ShapeDtypeStruct((BT, 1024), BF16),
                jax.ShapeDtypeStruct((64, per), BF16),
            ),
            in_specs=[pl.BlockSpec(memory_space=pltpu.HBM)] * 7,
            out_specs=(hbm, vmem),
            scratch_shapes=[
                pltpu.SMEM((NB,), jnp.int32),
                pltpu.SMEM((TOK,), jnp.int32),
                pltpu.VMEM((TOK, 1024), BF16),
                pltpu.VMEM((BT, 1024), BF16),
                pltpu.VMEM((BT, 2 * HEAD), BF16),
                pltpu.VMEM((BT, 2 * HEAD), BF16),
                pltpu.VMEM((2, BT, 512), BF16),
                pltpu.VMEM((2, BT, 2 * HEAD), BF16),
                pltpu.VMEM((2, BT, 2 * HEAD), BF16),
                pltpu.VMEM((2, BT, 2 * HEAD), BF16),
                pltpu.VMEM((2, BT, 2 * HEAD), BF16),
                pltpu.VMEM((2, ROWS, BT), F32),
                pltpu.VMEM((8, ROWS, 2 * HEAD), F32),
                pltpu.VMEM((8, ROWS, HEAD), F32),
                pltpu.VMEM((NZ, 2, PIECE, HEAD), BF16),
                pltpu.VMEM(pieces, BF16),
                pltpu.VMEM(pieces, BF16),
                pltpu.VMEM((NX, NZ, NY, 1, HEAD), jnp.int32),
                pltpu.VMEM((NX, NZ, NY, 1, HEAD), jnp.int32),
                pltpu.VMEM(anchor, BF16),
                pltpu.VMEM((NZ, BT // NZ, 2 * HEAD), BF16),
                pltpu.VMEM((NY, NX, NZ, PIECE, HEAD), BF16),
                pltpu.VMEM((NX, NZ, NY, PIECE, HEAD), BF16),
                pltpu.VMEM((NY, TOK, HEAD), F32),
                pltpu.VMEM((NX, NY, TOK, HEAD), F32),
                pltpu.VMEM((NX * NY, NZ, PIECE, HEAD), BF16),
                pltpu.VMEM((NX * NY, TOK, HEAD), F32),
                pltpu.VMEM((NX * NY, NZ, PIECE, HEAD), BF16),
                pltpu.VMEM((NX * NY, TOK, HEAD), F32),
                pltpu.VMEM((NZ, 2, PIECE, HEAD), BF16),
                pltpu.VMEM((TOK, HEAD), F32),
                pltpu.VMEM((NZ - 1, 2, PIECE, HEAD), BF16),
                pltpu.VMEM((NZ - 1, TOK, HEAD), F32),
                pltpu.VMEM((NZ, 2, PIECE, HEAD), BF16),
                pltpu.VMEM((NX, NY, 64, 1024), BF16),
                pltpu.VMEM((NX * NY, NT // NX, NZ * NX // NT * TOK // 2, HEAD), BF16),
                pltpu.VMEM((NY, NT, NZ * NX // NT * TOK // 2, HEAD), BF16),
                pltpu.SemaphoreType.DMA((240,)),
                pltpu.SemaphoreType.DMA((240,)),
                pltpu.SemaphoreType.DMA((9,)),
            ],
            compiler_params=pltpu.CompilerParams(
                collective_id=0, has_side_effects=True, vmem_limit_bytes=vlim * 2**20
            ),
            name="star_attention",
        )
        arrays = (lengths, positions, q, k, v, q_scored, weight.T)
        context_out, scored_t = call(*[pltpu.with_memory_space_constraint(a, pltpu.HBM) for a in arrays])
        return context_out, scored_t.T

    in_specs = (P("blk", "tp"), P("blk", "tp"), P("blk", "tp"), P(), P("blk", "tp"), P("blk"), P("tp", "blk"))
    out_specs = (P("blk", "tp"), P("tp", "blk"))
    return jax.shard_map(local, mesh=mesh, in_specs=in_specs, out_specs=out_specs, check_vma=False)
```
